32 devices in a mesh: grp: 2 (over y), anim: 8 (over z, x), mark: 2 (over core).
Axes of the slice: x: 2, y: 2, z: 4, core: 2. Of those that a mesh axis runs over, the one named last changes fastest.
Arguments:
- noncore_geno: int32 [2048, 512], P(('grp', 'anim'), 'mark'), parts along dimension 0, may hold values from 0 to 2
- noncore_codes: int32 [5, 2048], P(None, ('grp', 'anim')), parts along dimension 1, may hold values from 0 to 32, as said below
- core_geno: int32 [8192, 512], P('anim', 'mark'), may hold values from 0 to 2
- core_codes: int32 [5, 8192], P(None, 'anim'), may hold values from 0 to 32, as said below
- breed_freqs: float32 [5, 512], P(None, 'mark'), may hold values from 0.05 to 0.95
- core_inverse: bfloat16 [8192, 8192], P(None, 'anim'), may hold values from -0.25 to 0.25
Outputs:
- kinship_entries: bfloat16 [2048, 8192], P(('grp', 'anim'), 'mark'), parts along dimension 0
- inverse_weighted_kinship: bfloat16 [2048, 8192], P(('grp', 'anim'), 'mark'), parts along dimension 0
The draws below stay inside these ranges and needn't reach their ends.
There are 2 independent parts, one for each index of `grp`. The reference program is written for one: setup_inputs(seed, part) draws one part's arguments, and reference() takes and returns one part's arrays. A program takes and returns all parts, laid end to end along the dimension named above; an argument that names none is the same for every part. Nothing has to cross between parts.
Inputs may be any that keep to these rules, and one draw needn't show every extreme that they name: `noncore_codes`: each animal's 5 codes sum to 32. `core_codes`: each animal's 5 codes sum to 32.
All inputs are finite; a program needn't handle non-finite values.
Results may differ from the reference program's by a relative error of at most 0.0055.
Values may be sent and summed in bfloat16 or wider, within the bound.
No kernel may reach another device: no remote copies, remote signals or barrier semaphores. Data moves between devices by JAX's collectives and lax.ppermute only.
A program may use at most 64 MiB of HBM per device.

```python
import math
import jax
import jax.numpy as jnp
from jax import lax

BREEDS = 5
PROVEN_INDIVIDS = 8192
SLAB_MARKERS = 512
YOUNG_INDIVIDS = 1024
N_MARK = 2


def mixture_codes(key, count):
    cuts = jax.random.randint(key, (BREEDS - 1, count), 0, 33)
    cuts = jnp.sort(cuts, axis=0)
    edges = jnp.concatenate([jnp.zeros((1, count), jnp.int32), cuts.astype(jnp.int32), jnp.full((1, count), 32, jnp.int32)], 0)
    proportions = edges[1:] - edges[:-1]
    purebred = (jnp.arange(BREEDS)[:, None] == 0).astype(jnp.int32) * 32
    leading = jnp.arange(count)[None, :] == 0
    return jnp.where(leading, purebred, proportions).astype(jnp.int32)


def draw_noncore_codes(key, part):
    return mixture_codes(jax.random.fold_in(key, 11), YOUNG_INDIVIDS)


def draw_core_codes(key, part):
    return mixture_codes(jax.random.fold_in(key, 23), PROVEN_INDIVIDS)


def with_ends(array, own_key, least, top_value):
    spot = [jax.random.randint(jax.random.fold_in(own_key, axis), (), 0, length) for axis, length in enumerate(array.shape)]
    main_axis = array.shape.index(max(array.shape))
    beside = spot[:main_axis] + [(spot[main_axis] + 1) % array.shape[main_axis]] + spot[main_axis + 1:]
    return array.at[tuple(spot)].set(least).at[tuple(beside)].set(top_value)


def block_scale(stream_key, shape, pieces, smallest, high):
    def one(dim, shards_of):
        heights = jax.random.uniform(jax.random.fold_in(jax.random.fold_in(stream_key, 6), dim), (shards_of,), jnp.float32, smallest / len(pieces), high / len(pieces))
        return jnp.repeat(jnp.exp(heights), shape[dim] // shards_of).reshape((-1,) + (1,) * (len(shape) - dim - 1))

    gain = one(*pieces[0])
    for cut in pieces[1:]:
        gain = gain * one(*cut)
    return gain


def noise(key, dims, scale, limit, pieces=(), kind=jnp.bfloat16):
    result = jax.random.normal(key, dims, jnp.float32) * scale
    if len(pieces) > 0:
        result = block_scale(key, dims, pieces, -0.22, 0.18) * result
    return jnp.clip(result, min=-limit, max=limit).astype(kind)


def setup_inputs(seed: int = 0, part: int = 0) -> dict:
    seeds = jax.random.split(jax.random.key(seed), 7)
    own_keys = jax.random.split(jax.random.fold_in(seeds[6], part), 7)
    noncore_geno = with_ends(jax.random.randint(own_keys[0], (YOUNG_INDIVIDS, SLAB_MARKERS), 0, 3), jax.random.fold_in(own_keys[0], 1), 0, 2).astype(jnp.int32)
    noncore_codes = draw_noncore_codes(jax.random.fold_in(jax.random.fold_in(seeds[6], part), 71), part)
    core_geno = with_ends(jax.random.randint(seeds[2], (PROVEN_INDIVIDS, SLAB_MARKERS), 0, 3), jax.random.fold_in(seeds[2], 1), 0, 2).astype(jnp.int32)
    core_codes = draw_core_codes(jax.random.fold_in(seeds[6], 71), part)
    breed_freqs = jnp.clip(0.05 + 0.9 * jax.random.uniform(seeds[4], (BREEDS, SLAB_MARKERS), jnp.float32) ** block_scale(seeds[4], (BREEDS, SLAB_MARKERS), ((1, 2),), -0.2, 0.2), 0.05, 0.95)
    core_inverse = noise(seeds[5], (PROVEN_INDIVIDS, PROVEN_INDIVIDS), (PROVEN_INDIVIDS // 16) ** -0.5, 0.25, ((1, 8),))
    return {"noncore_geno": noncore_geno, "noncore_codes": noncore_codes, "core_geno": core_geno, "core_codes": core_codes, "breed_freqs": breed_freqs, "core_inverse": core_inverse}


def centre_value(genotypes, breed_codes, breed_freqs):
    fractions = breed_codes.astype(jnp.float32) / 32.0
    expected = lax.dot_general(fractions, breed_freqs, (((0,), (0,)), ((), ())), precision=lax.Precision.HIGHEST)
    return (genotypes.astype(jnp.float32) - 2.0 * expected).astype(jnp.bfloat16)


def reference(noncore_geno, noncore_codes, core_geno, core_codes, breed_freqs, core_inverse):
    noncore_z = centre_value(noncore_geno, noncore_codes, breed_freqs)
    core_z = centre_value(core_geno, core_codes, breed_freqs)
    half_marks = SLAB_MARKERS // N_MARK
    loadings = []
    for half_index in range(N_MARK):
        window = core_z[:, half_index * half_marks:(half_index + 1) * half_marks]
        loadings.append(jnp.dot(window.T, core_inverse, preferred_element_type=jnp.float32).astype(jnp.bfloat16))
    block_rows = math.gcd(YOUNG_INDIVIDS, 1024)
    number_of_tiles = noncore_z.reshape(YOUNG_INDIVIDS // block_rows, block_rows, SLAB_MARKERS)

    def kinship_submatrix(block_z):
        relate_total = jnp.zeros((block_rows, PROVEN_INDIVIDS), jnp.float32)
        regress_total = jnp.zeros((block_rows, PROVEN_INDIVIDS), jnp.float32)
        for half_index in range(N_MARK):
            low = half_index * half_marks
            part_z = block_z[:, low:low + half_marks]
            relate_part = jnp.dot(part_z, core_z[:, low:low + half_marks].T, preferred_element_type=jnp.float32) / SLAB_MARKERS
            regress_part = jnp.dot(part_z, loadings[half_index], preferred_element_type=jnp.float32) / SLAB_MARKERS
            relate_total = relate_total + lax.optimization_barrier(relate_part.astype(jnp.bfloat16)).astype(jnp.float32)
            regress_total = regress_total + lax.optimization_barrier(regress_part.astype(jnp.bfloat16)).astype(jnp.float32)
        return relate_total.astype(jnp.bfloat16), regress_total.astype(jnp.bfloat16)

    kinship_entries, inverse_weighted_kinship = lax.map(kinship_submatrix, number_of_tiles)
    return kinship_entries.reshape(YOUNG_INDIVIDS, PROVEN_INDIVIDS), inverse_weighted_kinship.reshape(YOUNG_INDIVIDS, PROVEN_INDIVIDS)
```

```python
import functools

import jax
import jax.numpy as jnp
from jax import lax
from jax.experimental import pallas as pl
from jax.experimental.pallas import tpu as pltpu
from jax.sharding import PartitionSpec as P

AXES = ("grp", "anim", "mark")
VMEM_LIMIT = 48 * 1024 * 1024


def whole():
    return pl.BlockSpec(memory_space=pltpu.VMEM)


def params(**more):
    return pltpu.CompilerParams(vmem_limit_bytes=VMEM_LIMIT, **more)


def shape(dims, dtype=jnp.bfloat16):
    return jax.ShapeDtypeStruct(dims, dtype)


def expected_dot(left, right):
    return lax.dot_general(
        left, right, (((0,), (0,)), ((), ())), precision=lax.Precision.HIGHEST,
        preferred_element_type=jnp.float32,
    )


def matmul(left, right):
    return jnp.dot(left, right, preferred_element_type=jnp.float32)


def centre_value(genotypes, breed_codes, breed_freqs):
    fractions = breed_codes.astype(jnp.float32) / 32.0
    expected = expected_dot(fractions, breed_freqs)
    return (genotypes.astype(jnp.float32) - 2.0 * expected).astype(jnp.bfloat16)


def gather_body(noncore_geno, noncore_codes, core_geno, core_codes, breed_freqs, core_inverse, *, n_mark):
    slab = breed_freqs.shape[1] * n_mark
    noncore_z = centre_value(noncore_geno, noncore_codes, breed_freqs)
    core_z = centre_value(core_geno, core_codes, breed_freqs)
    shard_rows = lax.all_gather(core_z, "anim", axis=0, tiled=True)
    related = (
        lax.dot_general(
            noncore_z, shard_rows, (((1,), (1,)), ((), ())), preferred_element_type=jnp.float32
        )
        / slab
    )
    loading = lax.dot_general(
        shard_rows, core_inverse, (((0,), (0,)), ((), ())), preferred_element_type=jnp.float32
    ).astype(jnp.bfloat16)
    scores = matmul(noncore_z, lax.all_gather(loading, "anim", axis=1, tiled=True)) / slab
    return tuple(
        lax.psum_scatter(part.astype(jnp.bfloat16), "mark", scatter_dimension=1, tiled=True)
        for part in (related, scores)
    )


def centre_kernel(place, geno, codes, freqs, out):
    fractions = codes[...].astype(jnp.float32) / 32.0
    expected = expected_dot(freqs[...], fractions)
    dosage = geno[...].astype(jnp.float32).T
    out[...] = (dosage - 2.0 * expected).astype(jnp.bfloat16)


def centre_core(part, core_geno, core_codes, breed_freqs):
    rows, markers = core_geno.shape[0] // 2, core_geno.shape[1]
    breeds = core_codes.shape[0]
    return pl.pallas_call(
        centre_kernel,
        grid_spec=pltpu.PrefetchScalarGridSpec(
            num_scalar_prefetch=1,
            grid=(1,),
            in_specs=[
                pl.BlockSpec((rows, markers), lambda i, place: (place[0], 0)),
                pl.BlockSpec((breeds, rows), lambda i, place: (0, place[0])),
                pl.BlockSpec((breeds, markers), lambda i, place: (0, 0)),
            ],
            out_specs=pl.BlockSpec((markers, rows), lambda i, place: (0, 0)),
        ),
        out_shape=shape((markers, rows)),
        compiler_params=params(),
        name="centre_core",
    )(part[None], core_geno, core_codes, breed_freqs)


def loading_kernel(count, first, last, place, *refs):
    pieces, refs = refs[:count], refs[count:]
    inverse, refs = refs[0], refs[1:]
    if not first:
        before, refs = refs[0], refs[1:]
    if last:
        keep, send, total = refs
    else:
        (total,) = refs
    step = pl.program_id(0)
    for i in range(count):
        @pl.when(step == i)
        def _(i=i):
            product = matmul(pieces[i][...], inverse[...])
            if i > 0:
                total[...] += product
            elif first:
                total[...] = product
            else:
                total[...] = before[...] + product

    if last:
        @pl.when(step == count - 1)
        def _():
            half = keep.shape[1]
            mine = pl.ds(pl.multiple_of(place[count] * half, half), half)
            other = pl.ds(pl.multiple_of((1 - place[count]) * half, half), half)
            keep[...] = total[:, mine]
            send[...] = total[:, other].astype(jnp.bfloat16)


def add_loadings(pieces, blocks, part, core_inverse, before, last):
    count, (markers, rows), columns = len(pieces), pieces[0].shape, core_inverse.shape[1]
    first = before is None
    fixed = lambda i, place: (0, 0)
    in_specs = [pl.BlockSpec((markers, rows), fixed) for _ in pieces]
    in_specs.append(pl.BlockSpec((rows, columns), lambda i, place: (place[i], 0)))
    operands = list(pieces) + [core_inverse]
    if not first:
        in_specs.append(pl.BlockSpec((markers, columns), fixed))
        operands.append(before)
    if last:
        half = columns // 2
        out_shape = (shape((markers, half), jnp.float32), shape((markers, half)))
        out_specs = [pl.BlockSpec((markers, half), fixed)] * 2
        scratch = [pltpu.VMEM((markers, columns), jnp.float32)]
    else:
        out_shape = shape((markers, columns), jnp.float32)
        out_specs = pl.BlockSpec((markers, columns), fixed)
        scratch = []
    place = jnp.stack(list(blocks) + [part]).astype(jnp.int32)
    return pl.pallas_call(
        functools.partial(loading_kernel, count, first, last),
        grid_spec=pltpu.PrefetchScalarGridSpec(
            num_scalar_prefetch=1, grid=(count,), in_specs=in_specs, out_specs=out_specs,
            scratch_shapes=scratch,
        ),
        out_shape=out_shape,
        compiler_params=params(),
        cost_estimate=pl.CostEstimate(
            flops=2 * count * markers * rows * columns,
            bytes_accessed=2 * count * rows * (columns + markers) + 8 * markers * columns,
            transcendentals=0,
        ),
        name="add_loadings",
    )(place, *operands)


def relation_kernel(count, scale, place, noncore, *refs):
    pieces, (own, send) = refs[:count], refs[count:]
    width = pieces[0].shape[1]
    for k in range(count):
        value = (matmul(noncore[...], pieces[k][...]) * scale).astype(jnp.bfloat16)
        columns = pl.ds(pl.multiple_of(place[2 * k + 1] * width, width), width)

        @pl.when(place[2 * k] == 1)
        def _(value=value, columns=columns):
            own[:, columns] = value

        @pl.when(place[2 * k] == 0)
        def _(value=value, columns=columns):
            send[:, columns] = value


def relate(noncore, pieces, own_flags, slots, scale):
    count, width, rows = len(pieces), pieces[0].shape[1], noncore.shape[0]
    place = jnp.stack([v for pair in zip(own_flags, slots) for v in pair]).astype(jnp.int32)
    out = shape((rows, width * count // 2))
    return pl.pallas_call(
        functools.partial(relation_kernel, count, scale),
        in_specs=[pl.BlockSpec(memory_space=pltpu.SMEM)] + [whole()] * (count + 1),
        out_specs=(whole(), whole()),
        out_shape=(out, out),
        compiler_params=params(),
        cost_estimate=pl.CostEstimate(
            flops=2 * count * rows * width * noncore.shape[1],
            bytes_accessed=4 * count * width * rows,
            transcendentals=0,
        ),
        name="relate",
    )(place, noncore, *pieces)


def regression_kernel(count, scale, place, first, second, mine, other, *outs):
    rows = outs[0].shape[0]
    for k in range(count):
        block = pl.ds(pl.multiple_of(place[k] * rows, rows), rows)
        value = matmul(first[block, :], mine[...]) + matmul(second[block, :], other[...])
        outs[k][...] = (value * scale).astype(jnp.bfloat16)


def regress(first, second, mine, other, row_blocks, scale):
    count, width = len(row_blocks), mine.shape[1]
    rows = first.shape[0] // count
    return pl.pallas_call(
        functools.partial(regression_kernel, count, scale),
        in_specs=[pl.BlockSpec(memory_space=pltpu.SMEM)] + [whole()] * 4,
        out_specs=[whole()] * count,
        out_shape=[shape((rows, width))] * count,
        compiler_params=params(),
        cost_estimate=pl.CostEstimate(
            flops=4 * first.size * width, bytes_accessed=2 * (4 * first.size + 2 * mine.size),
            transcendentals=0,
        ),
        name="regress",
    )(jnp.stack(row_blocks).astype(jnp.int32), first, second, mine, other)


def assemble_kernel(width, place, *refs):
    parts, out = refs[:-1], refs[-1]
    slot = 0
    for part in parts:
        for start in range(0, part.shape[1], width):
            columns = pl.ds(pl.multiple_of(place[slot] * width, width), width)
            out[:, columns] = part[:, start:start + width]
            slot += 1


def assemble(parts, slots, width):
    rows = parts[0].shape[0]
    return pl.pallas_call(
        functools.partial(assemble_kernel, width),
        in_specs=[pl.BlockSpec(memory_space=pltpu.SMEM)] + [whole()] * len(parts),
        out_specs=whole(),
        out_shape=shape((rows, width * len(slots))),
        compiler_params=params(),
        name="assemble",
    )(jnp.stack(slots).astype(jnp.int32), *parts)


def permute_body(
    noncore_geno, noncore_codes, core_geno, core_codes, breed_freqs, core_inverse, *, n_anim, n_mark
):
    markers = breed_freqs.shape[1]
    scale = 1.0 / (markers * n_mark)
    top = n_anim // 2
    grp, anim, mark = (lax.axis_index(name) for name in AXES)

    def move(array, target):
        pairs = []
        for g in range(2):
            for a in range(n_anim):
                for m in range(2):
                    tg, ta, tm = target(g, a, m)
                    pairs.append(((g * n_anim + a) * 2 + m, (tg * n_anim + ta) * 2 + tm))
        return lax.ppermute(array, AXES, pairs)

    def along_anim(array, bits):
        return move(array, lambda g, a, m: (g, a ^ bits, m))

    def across_grp(array):
        return move(array, lambda g, a, m: (1 - g, a, m))

    def across_mark(array):
        return move(array, lambda g, a, m: (g, a, 1 - m))

    own = centre_core(grp, core_geno, core_codes, breed_freqs)
    pieces = {0: own}
    far = [top] + [b for b in range(2, n_anim, 2) if b != top]
    for bits in far:
        pieces[bits] = along_anim(own, bits)
    pieces[1] = along_anim(own, 1)
    for bits in far:
        pieces[bits + 1] = along_anim(pieces[bits], 1)

    noncore_z = centre_value(noncore_geno, noncore_codes, breed_freqs)
    both = jnp.concatenate([noncore_z, across_grp(noncore_z)], axis=0)
    gathered = noncore_z
    bit = 1
    while bit < n_anim:
        gathered = jnp.concatenate([gathered, along_anim(gathered, bit)], axis=0)
        bit *= 2
    one = move(gathered, lambda g, a, m: (1 - g, a, m) if m == g else (g, a, 1 - m))
    two = move(gathered, lambda g, a, m: (1 - g, a, 1 - m))
    at_home = mark == grp
    first = jnp.where(at_home, gathered, one)
    second = jnp.where(at_home, one, two)

    early = [0, 1] + [b for b in far[:1]]
    late = [b for b in range(n_anim) if b not in early]
    block = lambda bits: (anim ^ bits) * 2 + grp
    total = add_loadings(
        [pieces[b] for b in early], [block(b) for b in early], grp, core_inverse, None, False
    )
    keep, send = add_loadings(
        [pieces[b] for b in late], [block(b) for b in late], grp, core_inverse, total, True
    )
    mine = (keep + across_grp(send).astype(jnp.float32)).astype(jnp.bfloat16)
    other = across_mark(mine)

    high = (anim // top) ^ grp
    row_blocks = [(high ^ (k // top)) * top + k % top for k in range(n_anim)]
    results = regress(first, second, mine, other, row_blocks, scale)
    arrived = [
        move(
            results[k],
            lambda g, a, m, k=k: (m, (g * top + a % top) ^ k, a // top),
        )
        for k in range(n_anim)
    ]
    slots = [((anim ^ k) % top) * 2 + (anim ^ k) // top for k in range(n_anim)]
    weighted = assemble(arrived, slots, own.shape[1])

    own_part, send_part = relate(
        both,
        [pieces[k] for k in range(n_anim)],
        [((anim ^ k) // top == mark).astype(jnp.int32) for k in range(n_anim)],
        [(anim ^ k) % top for k in range(n_anim)],
        scale,
    )
    summed = (
        own_part.astype(jnp.float32) + across_mark(send_part).astype(jnp.float32)
    ).astype(jnp.bfloat16)
    rows = noncore_z.shape[0]
    kept, from_other = summed[:rows], across_grp(summed[rows:])
    slots = [2 * i + grp for i in range(top)] + [2 * i + 1 - grp for i in range(top)]
    kinship = assemble([kept, from_other], slots, own.shape[1])
    return kinship, weighted


def solution(mesh):
    in_specs = (
        P(("grp", "anim"), "mark"),
        P(None, ("grp", "anim")),
        P("anim", "mark"),
        P(None, "anim"),
        P(None, "mark"),
        P(None, "anim"),
    )
    out_specs = (P(("grp", "anim"), "mark"), P(("grp", "anim"), "mark"))
    n_grp, n_anim, n_mark = (mesh.shape[name] for name in AXES)
    if n_grp == 2 and n_mark == 2 and n_anim in (4, 8, 16):
        body = functools.partial(permute_body, n_anim=n_anim, n_mark=n_mark)
    else:
        body = functools.partial(gather_body, n_mark=n_mark)
    return jax.shard_map(body, mesh=mesh, in_specs=in_specs, out_specs=out_specs, check_vma=False)
```

```python
import functools

import jax
import jax.numpy as jnp
from jax import lax
from jax.experimental import pallas as pl
from jax.experimental.pallas import tpu as pltpu
from jax.sharding import PartitionSpec as P

AXES = ("grp", "anim", "mark")
VMEM_LIMIT = 16 * 1024 * 1024
PARTS = 2
SHORT = pl.CostEstimate(flops=0, bytes_accessed=0, transcendentals=0)


def whole():
    return pl.BlockSpec(memory_space=pltpu.VMEM)


def anywhere():
    return pl.BlockSpec(memory_space=pl.ANY)


def in_hbm(array):
    return pltpu.with_memory_space_constraint(array, pltpu.HBM)


def params(**more):
    return pltpu.CompilerParams(vmem_limit_bytes=VMEM_LIMIT, **more)


def shape(dims, dtype=jnp.bfloat16):
    return jax.ShapeDtypeStruct(dims, dtype)


def expected_dot(left, right):
    return lax.dot_general(
        left, right, (((0,), (0,)), ((), ())), precision=lax.Precision.HIGHEST,
        preferred_element_type=jnp.float32,
    )


def matmul(left, right):
    return jnp.dot(left, right, preferred_element_type=jnp.float32)


def centre_value(genotypes, breed_codes, breed_freqs):
    fractions = breed_codes.astype(jnp.float32) / 32.0
    expected = expected_dot(fractions, breed_freqs)
    return (genotypes.astype(jnp.float32) - 2.0 * expected).astype(jnp.bfloat16)


def gather_body(noncore_geno, noncore_codes, core_geno, core_codes, breed_freqs, core_inverse, *, n_mark):
    slab = breed_freqs.shape[1] * n_mark
    noncore_z = centre_value(noncore_geno, noncore_codes, breed_freqs)
    core_z = centre_value(core_geno, core_codes, breed_freqs)
    shard_rows = lax.all_gather(core_z, "anim", axis=0, tiled=True)
    related = (
        lax.dot_general(
            noncore_z, shard_rows, (((1,), (1,)), ((), ())), preferred_element_type=jnp.float32
        )
        / slab
    )
    loading = lax.dot_general(
        shard_rows, core_inverse, (((0,), (0,)), ((), ())), preferred_element_type=jnp.float32
    ).astype(jnp.bfloat16)
    scores = matmul(noncore_z, lax.all_gather(loading, "anim", axis=1, tiled=True)) / slab
    return tuple(
        lax.psum_scatter(part.astype(jnp.bfloat16), "mark", scatter_dimension=1, tiled=True)
        for part in (related, scores)
    )


def centre_kernel(
    place, geno, codes, freqs, noncore_geno, noncore_codes, piece, noncore, *scratch
):
    rows, markers = geno.shape[0] // 2, geno.shape[1]
    mine = pl.ds(pl.multiple_of(place[0] * rows, rows), rows)
    here, sem = scratch[:-1], scratch[-1]
    sources = [codes, freqs, noncore_codes, noncore_geno, geno.at[mine, :]]
    copies = [
        pltpu.make_async_copy(source, target, sem.at[i])
        for i, (source, target) in enumerate(zip(sources, here))
    ]
    for copy in copies:
        copy.start()
    for copy in copies[:3]:
        copy.wait()
    codes, freqs, noncore_codes, noncore_geno, geno = here
    expected = expected_dot(freqs[...], codes[:, mine].astype(jnp.float32) / 32.0)
    noncore_expected = expected_dot(noncore_codes[...].astype(jnp.float32) / 32.0, freqs[...])
    copies[3].wait()
    centred = (noncore_geno[...].astype(jnp.float32) - 2.0 * noncore_expected).astype(jnp.bfloat16)
    noncore[...] = centred
    height = piece.shape[0] - markers
    for i in range(rows // markers):
        piece[markers:, i * markers:(i + 1) * markers] = centred[i * height:(i + 1) * height, :]
    copies[4].wait()
    dosage = geno[...].astype(jnp.float32).T
    piece[:markers, :] = (dosage - 2.0 * expected).astype(jnp.bfloat16)


def centre(part, core_geno, core_codes, breed_freqs, noncore_geno, noncore_codes):
    rows, markers = core_geno.shape[0] // 2, core_geno.shape[1]
    noncore = noncore_geno.shape[0]
    operands = [core_geno, core_codes, breed_freqs, noncore_geno, noncore_codes]
    return pl.pallas_call(
        centre_kernel,
        in_specs=[pl.BlockSpec(memory_space=pltpu.SMEM)] + [anywhere()] * 5,
        out_specs=[whole()] * 2,
        out_shape=[shape((markers + noncore * markers // rows, rows)), shape((noncore, markers))],
        scratch_shapes=[
            pltpu.VMEM(core_codes.shape, jnp.int32),
            pltpu.VMEM(breed_freqs.shape, jnp.float32),
            pltpu.VMEM(noncore_codes.shape, jnp.int32),
            pltpu.VMEM(noncore_geno.shape, jnp.int32),
            pltpu.VMEM((rows, markers), jnp.int32),
            pltpu.SemaphoreType.DMA((5,)),
        ],
        compiler_params=params(),
        cost_estimate=SHORT,
        name="centre",
    )(part[None], *[in_hbm(operand) for operand in operands])


def unfold_kernel(count, flag, *refs):
    markers = refs[-1].shape[1]
    pieces, outs = refs[:-2], refs[-2:]
    height = pieces[0].shape[0] - markers
    folds = pieces[0].shape[1] // markers
    for b in range(count):
        for i in range(folds):
            spot = slice((b * folds + i) * height, (b * folds + i + 1) * height)
            for j in range(2):
                @pl.when(flag[0] == j)
                def _(b=b, i=i, j=j, spot=spot):
                    for k in range(2):
                        piece = pieces[b + count * (j ^ k)]
                        outs[k][spot, :] = piece[markers:, i * markers:(i + 1) * markers]


def unfold(pieces, noncore_shape, flag):
    rows, markers = noncore_shape
    count = len(pieces) // 2
    return pl.pallas_call(
        functools.partial(unfold_kernel, count),
        in_specs=[pl.BlockSpec(memory_space=pltpu.SMEM)] + [whole()] * len(pieces),
        out_specs=[whole()] * 2,
        out_shape=[shape((rows * count, markers))] * 2,
        compiler_params=params(),
        cost_estimate=SHORT,
        name="unfold",
    )(flag.astype(jnp.int32)[None], *pieces)


def absorb_kernel(count, pairs, ahead, first, scale, place, *refs):
    refs = list(refs)
    pieces = [refs.pop(0) for _ in range(count)]
    inverse = refs.pop(0)
    related = [(refs.pop(0), refs.pop(0)) for _ in range(pairs)]
    noncore = refs.pop(0) if pairs else None
    before = None if first else refs.pop(0)
    fetched = inverse.ndim == 3
    slabs, sem = (inverse, None) if fetched else refs[-2:]
    outs = refs if fetched else refs[:-2]
    later = outs.pop() if ahead else None
    own, send = (outs.pop(-2), outs.pop(-1)) if pairs else (None, None)
    rows, columns = pieces[0].shape[1], inverse.shape[-1]

    copies = []
    for i in range(0 if fetched else count + ahead):
        block = pl.ds(pl.multiple_of(place[i] * rows, rows), rows)
        target = slabs.at[i] if i < count else later.at[i - count]
        copies.append(pltpu.make_async_copy(inverse.at[block, :], target, sem.at[i]))
        copies[-1].start()
    for i, pair in enumerate(related):
        values = [
            (matmul(noncore[...], p[:noncore.shape[1], :]) * scale).astype(jnp.bfloat16)
            for p in pair
        ]
        for j in range(2):
            @pl.when(place[count + ahead] == j)
            def _(i=i, j=j, values=values):
                own[:, i * rows:(i + 1) * rows] = values[j]
                send[:, i * rows:(i + 1) * rows] = values[1 - j]

    for copy in copies[:count]:
        copy.wait()
    for start in range(0, columns, 256):
        part = slice(start, start + 256)
        total = None if first else before[:, part]
        for i in range(count):
            product = matmul(pieces[i][:outs[0].shape[0], :], slabs[i, :, part])
            total = product if total is None else total + product
        outs[0][:, part] = total
        for i, out in enumerate(outs[1:]):
            width = out.shape[1]
            if i * width <= start < (i + 1) * width:
                out[:, start - i * width:start - i * width + 256] = total.astype(out.dtype)
    for copy in copies[count:]:
        copy.wait()


def absorb(pieces, blocks, inverse, before, noncore, pairs, flag, scale, parts=0):
    count, rows, columns, markers = len(pieces), pieces[0].shape[1], inverse.shape[-1], noncore.shape[1]
    ahead, fetched = len(blocks) - count, inverse.ndim == 3
    operands = [*pieces, inverse] + [piece for pair in pairs for piece in pair]
    operands += [noncore] if pairs else []
    operands += [] if before is None else [before]
    outs = [shape((markers, columns), jnp.float32)]
    outs += [shape((markers, columns // parts)) for _ in range(parts)]
    outs += [shape((noncore.shape[0], rows * len(pairs)))] * 2 if pairs else []
    outs += [shape((ahead, rows, columns))] if ahead else []
    specs = [whole()] * len(operands)
    specs[count] = whole() if fetched else anywhere()
    return pl.pallas_call(
        functools.partial(absorb_kernel, count, len(pairs), ahead, before is None, scale),
        in_specs=[pl.BlockSpec(memory_space=pltpu.SMEM)] + specs,
        out_specs=[whole()] * len(outs),
        out_shape=outs,
        scratch_shapes=[] if fetched else [
            pltpu.VMEM((count, rows, columns), jnp.bfloat16),
            pltpu.SemaphoreType.DMA((count + ahead,)),
        ],
        compiler_params=params(),
        cost_estimate=SHORT,
        name="absorb",
    )(jnp.stack(blocks + [flag]).astype(jnp.int32), *operands)


def add_kernel(start, total, other, out):
    width = out.shape[1]
    out[...] = (total[:, start:start + width] + other[...].astype(jnp.float32)).astype(out.dtype)


def add_part(total, other, start):
    return pl.pallas_call(
        functools.partial(add_kernel, start),
        in_specs=[whole()] * 2,
        out_specs=whole(),
        out_shape=shape(other.shape),
        compiler_params=params(),
        cost_estimate=SHORT,
        name="add_part",
    )(total, other)


def relation_kernel(count, scale, flag, done, noncore, *refs):
    pieces, (own, send) = refs[:2 * count], refs[2 * count:]
    width = pieces[0].shape[1]
    for i in range(count):
        columns = slice(i * width, (i + 1) * width)
        values = [
            (matmul(noncore[...], pieces[2 * i + j][:noncore.shape[1], :]) * scale).astype(jnp.bfloat16)
            for j in range(2)
        ]
        for j in range(2):
            @pl.when(flag[0] == j)
            def _(j=j):
                own[:, columns] = values[j]
                send[:, columns] = values[1 - j]


def relate(noncore, pairs, flag, scale, after):
    rows, width = noncore.shape[0], pairs[0][0].shape[1]
    out = shape((rows, width * len(pairs)))
    return pl.pallas_call(
        functools.partial(relation_kernel, len(pairs), scale),
        in_specs=[pl.BlockSpec(memory_space=pltpu.SMEM), anywhere()]
        + [whole()] * (2 * len(pairs) + 1),
        out_specs=(whole(), whole()),
        out_shape=(out, out),
        compiler_params=params(),
        cost_estimate=SHORT,
        name="relate",
    )(flag.astype(jnp.int32)[None], after, noncore, *[piece for pair in pairs for piece in pair])


def regression_kernel(count, scale, kept, got, mine, other, *outs):
    rows = outs[0].shape[0]
    for k in range(count):
        block = slice(k * rows, (k + 1) * rows)
        value = matmul(kept[block, :], mine[...]) + matmul(got[block, :], other[...])
        outs[k][...] = (value * scale).astype(jnp.bfloat16)


def regress(kept, got, mine, other, count, scale):
    rows, width = kept.shape[0] // count, mine.shape[1]
    return pl.pallas_call(
        functools.partial(regression_kernel, count, scale),
        in_specs=[whole()] * 4,
        out_specs=[whole()] * count,
        out_shape=[shape((rows, width))] * count,
        compiler_params=params(),
        cost_estimate=SHORT,
        name="regress",
    )(kept, got, mine, other)


def assemble_kernel(jobs, place, *refs):
    refs, sem = list(refs[:-1]), refs[-1]
    outs = refs[-len(jobs):]
    copies = []
    for (count, width), out in zip(jobs, outs):
        for _ in range(count):
            part = refs.pop(0)
            for start in range(0, part.shape[1], width):
                slot = len(copies)
                columns = pl.ds(pl.multiple_of(place[slot] * width, width), width)
                copies.append(
                    pltpu.make_async_copy(
                        part.at[:, start:start + width], out.at[:, columns], sem.at[slot]
                    )
                )
                copies[-1].start()
    for copy in copies:
        copy.wait()


def assemble(jobs):
    parts = [part for job in jobs for part in job[0]]
    slots = [slot for job in jobs for slot in job[1]]
    return pl.pallas_call(
        functools.partial(assemble_kernel, [(len(job[0]), job[2]) for job in jobs]),
        in_specs=[pl.BlockSpec(memory_space=pltpu.SMEM)] + [anywhere()] * len(parts),
        out_specs=[anywhere()] * len(jobs),
        out_shape=[shape((job[0][0].shape[0], job[2] * len(job[1]))) for job in jobs],
        scratch_shapes=[pltpu.SemaphoreType.DMA((len(slots),))],
        compiler_params=params(),
        cost_estimate=SHORT,
        name="assemble",
    )(jnp.stack(slots).astype(jnp.int32), *parts)


def permute_body(
    noncore_geno, noncore_codes, core_geno, core_codes, breed_freqs, core_inverse, *, n_anim, n_mark
):
    markers = breed_freqs.shape[1]
    scale = 1.0 / (markers * n_mark)
    top = n_anim // 2
    grp, anim, mark = (lax.axis_index(name) for name in AXES)

    def move(array, target):
        pairs = []
        for g in range(2):
            for a in range(n_anim):
                for m in range(2):
                    tg, ta, tm = target(g, a, m)
                    pairs.append(((g * n_anim + a) * 2 + m, (tg * n_anim + ta) * 2 + tm))
        return lax.ppermute(array, AXES, pairs)

    def along_anim(array, bits):
        return move(array, lambda g, a, m: (g, a ^ bits, m))

    def across_grp(array):
        return move(array, lambda g, a, m: (1 - g, a, m))

    def across_mark(array):
        return move(array, lambda g, a, m: (g, a, 1 - m))

    own, noncore = centre(
        grp, core_geno, core_codes, breed_freqs, noncore_geno, noncore_codes
    )
    rows = noncore.shape[0]
    both = jnp.concatenate([noncore, across_grp(noncore)], axis=0)
    at_home = mark == anim // top
    flag = jnp.where(at_home, 0, 1)
    inverse = in_hbm(core_inverse)
    pieces, related = {0: own}, []

    def take(chosen, total, pairs=(), ahead=(), parts=0, rows_of=inverse):
        result = absorb(
            [pieces[b] for b in chosen], [(anim ^ b) * 2 + grp for b in [*chosen, *ahead]], rows_of,
            total, both, [(pieces[b], pieces[b + top]) for b in pairs], flag, scale, parts,
        )
        if pairs:
            related.extend(result[1 + parts:3 + parts])
        return [result[0], *result[1:1 + parts]] + list(result[3 + parts if pairs else 1 + parts:])

    low = list(range(2, top, 2))
    for bits in low + [top, 1]:
        pieces[bits] = along_anim(own, bits)
    for bits in low:
        pieces[bits + 1] = along_anim(pieces[bits], 1)
    held = [top, 1] + [b + 1 for b in low]
    for b, piece in zip(held, lax.optimization_barrier([pieces[b] for b in held])):
        pieces[b] = piece
    for bits in low:
        pieces[top + bits] = along_anim(pieces[top], bits)
    for bits in [0] + low:
        pieces[top + bits + 1] = along_anim(pieces[top + bits], 1)
    (total,) = take([0, 1] + low, None)
    last = [top + bits + i for bits in low for i in range(2)]
    total, slabs = take([b + 1 for b in low] + [top, top + 1], total, [0, 1], last)
    total, *send = take(last, total, parts=PARTS, rows_of=slabs)

    kept, got = unfold([pieces[b] for b in range(n_anim)], noncore.shape, flag)
    got = across_mark(got)
    from_other = [across_grp(part) for part in send]

    arrived, slots = [], []
    for i, part in enumerate(from_other):
        width = part.shape[1]
        mine = add_part(total, part, i * width)
        other = across_mark(mine)
        if i + 1 < PARTS:
            other, from_other[i + 1] = lax.optimization_barrier((other, from_other[i + 1]))
        results = regress(kept, got, mine, other, top, scale)
        if i == 0:
            begun = results[0]
        for k in range(top):
            arrived.append(
                move(results[k], lambda g, a, m, k=k: (g, m * top + (a % top ^ k), a // top))
            )
            slots.append((anim ^ k) % top * PARTS + i)

    related += relate(both, [(pieces[b - top], pieces[b]) for b in last], flag, scale, begun)
    received = [across_mark(part) for part in related[1::2]]
    sums = [
        jnp.concatenate(
            [
                (mine[part].astype(jnp.float32) + yours[part].astype(jnp.float32)).astype(
                    jnp.bfloat16
                )
                for mine, yours in zip(related[::2], received)
            ],
            axis=1,
        )
        for part in (slice(0, rows), slice(rows, 2 * rows))
    ]
    swapped = across_grp(sums[1])

    width_of_piece = own.shape[1]
    order = [0, 1] + [b - top for b in last]
    places = [2 * ((anim ^ b) % top) + g for g in (grp, 1 - grp) for b in order]
    return tuple(
        assemble([([sums[0], swapped], places, width_of_piece), (arrived, slots, width)])
    )


def solution(mesh):
    in_specs = (
        P(("grp", "anim"), "mark"),
        P(None, ("grp", "anim")),
        P("anim", "mark"),
        P(None, "anim"),
        P(None, "mark"),
        P(None, "anim"),
    )
    out_specs = (P(("grp", "anim"), "mark"), P(("grp", "anim"), "mark"))
    n_grp, n_anim, n_mark = (mesh.shape[name] for name in AXES)
    if n_grp == 2 and n_mark == 2 and n_anim in (8, 16):
        body = functools.partial(permute_body, n_anim=n_anim, n_mark=n_mark)
    else:
        body = functools.partial(gather_body, n_mark=n_mark)
    return jax.shard_map(body, mesh=mesh, in_specs=in_specs, out_specs=out_specs, check_vma=False)
```

```python
import functools

import jax
import jax.numpy as jnp
from jax import lax
from jax.experimental import pallas as pl
from jax.experimental.pallas import tpu as pltpu
from jax.sharding import PartitionSpec as P

AXES = ("grp", "anim", "mark")
VMEM_LIMIT = 16 * 1024 * 1024
SHORT = pl.CostEstimate(flops=0, bytes_accessed=0, transcendentals=0)


def whole():
    return pl.BlockSpec(memory_space=pltpu.VMEM)


def anywhere():
    return pl.BlockSpec(memory_space=pl.ANY)


def in_hbm(array):
    return pltpu.with_memory_space_constraint(array, pltpu.HBM)


def params(**more):
    return pltpu.CompilerParams(vmem_limit_bytes=VMEM_LIMIT, **more)


def shape(dims, dtype=jnp.bfloat16):
    return jax.ShapeDtypeStruct(dims, dtype)


def expected_dot(left, right):
    return lax.dot_general(
        left, right, (((0,), (0,)), ((), ())), precision=lax.Precision.HIGHEST,
        preferred_element_type=jnp.float32,
    )


def matmul(left, right):
    return jnp.dot(left, right, preferred_element_type=jnp.float32)


def centre_value(genotypes, breed_codes, breed_freqs):
    fractions = breed_codes.astype(jnp.float32) / 32.0
    expected = expected_dot(fractions, breed_freqs)
    return (genotypes.astype(jnp.float32) - 2.0 * expected).astype(jnp.bfloat16)


def gather_body(noncore_geno, noncore_codes, core_geno, core_codes, breed_freqs, core_inverse, *, n_mark):
    slab = breed_freqs.shape[1] * n_mark
    noncore_z = centre_value(noncore_geno, noncore_codes, breed_freqs)
    core_z = centre_value(core_geno, core_codes, breed_freqs)
    shard_rows = lax.all_gather(core_z, "anim", axis=0, tiled=True)
    related = (
        lax.dot_general(
            noncore_z, shard_rows, (((1,), (1,)), ((), ())), preferred_element_type=jnp.float32
        )
        / slab
    )
    loading = lax.dot_general(
        shard_rows, core_inverse, (((0,), (0,)), ((), ())), preferred_element_type=jnp.float32
    ).astype(jnp.bfloat16)
    scores = matmul(noncore_z, lax.all_gather(loading, "anim", axis=1, tiled=True)) / slab
    return tuple(
        lax.psum_scatter(part.astype(jnp.bfloat16), "mark", scatter_dimension=1, tiled=True)
        for part in (related, scores)
    )


def centre_kernel(
    place, geno, codes, freqs, noncore_geno, noncore_codes, piece, noncore, *scratch
):
    rows, markers = geno.shape[0] // 2, geno.shape[1]
    mine = pl.ds(pl.multiple_of(place[0] * rows, rows), rows)
    here, sem = scratch[:-1], scratch[-1]
    sources = [codes, freqs, noncore_codes, noncore_geno, geno.at[mine, :]]
    copies = [
        pltpu.make_async_copy(source, target, sem.at[i])
        for i, (source, target) in enumerate(zip(sources, here))
    ]
    for copy in copies:
        copy.start()
    for copy in copies[:3]:
        copy.wait()
    codes, freqs, noncore_codes, noncore_geno, geno = here
    expected = expected_dot(freqs[...], codes[:, mine].astype(jnp.float32) / 32.0)
    noncore_expected = expected_dot(noncore_codes[...].astype(jnp.float32) / 32.0, freqs[...])
    copies[3].wait()
    centred = (noncore_geno[...].astype(jnp.float32) - 2.0 * noncore_expected).astype(jnp.bfloat16)
    noncore[...] = centred
    copies[4].wait()
    dosage = geno[...].astype(jnp.float32).T
    piece[...] = (dosage - 2.0 * expected).astype(jnp.bfloat16)


def centre(part, core_geno, core_codes, breed_freqs, noncore_geno, noncore_codes):
    rows, markers = core_geno.shape[0] // 2, core_geno.shape[1]
    noncore = noncore_geno.shape[0]
    operands = [core_geno, core_codes, breed_freqs, noncore_geno, noncore_codes]
    return pl.pallas_call(
        centre_kernel,
        in_specs=[pl.BlockSpec(memory_space=pltpu.SMEM)] + [anywhere()] * 5,
        out_specs=[whole()] * 2,
        out_shape=[shape((markers, rows)), shape((noncore, markers))],
        scratch_shapes=[
            pltpu.VMEM(core_codes.shape, jnp.int32),
            pltpu.VMEM(breed_freqs.shape, jnp.float32),
            pltpu.VMEM(noncore_codes.shape, jnp.int32),
            pltpu.VMEM(noncore_geno.shape, jnp.int32),
            pltpu.VMEM((rows, markers), jnp.int32),
            pltpu.SemaphoreType.DMA((5,)),
        ],
        compiler_params=params(),
        cost_estimate=SHORT,
        name="centre",
    )(part[None], *[in_hbm(operand) for operand in operands])


def absorb_kernel(count, pairs, ahead, first, scale, place, *refs):
    refs = list(refs)
    pieces = [refs.pop(0) for _ in range(count)]
    inverse = refs.pop(0)
    related = [(refs.pop(0), refs.pop(0)) for _ in range(pairs)]
    noncore = refs.pop(0) if pairs else None
    before = None if first else refs.pop(0)
    fetched = inverse.ndim == 3
    slabs, sem = (inverse, None) if fetched else refs[-2:]
    outs = refs if fetched else refs[:-2]
    later = outs.pop() if ahead else None
    own, send = (outs.pop(-2), outs.pop(-1)) if pairs else (None, None)
    rows, columns = pieces[0].shape[1], inverse.shape[-1]

    copies = []
    half = columns // 2
    for i in range(0 if fetched else count + ahead):
        block = pl.ds(pl.multiple_of(place[i] * rows, rows), rows)
        target = slabs.at[i] if i < count else later.at[i - count]
        for j, side in enumerate((place[count + ahead + 1], 1 - place[count + ahead + 1])):
            source = inverse.at[block, pl.ds(pl.multiple_of(side * half, half), half)]
            copies.append(
                pltpu.make_async_copy(
                    source, target.at[:, j * half:(j + 1) * half], sem.at[2 * i + j]
                )
            )
            copies[-1].start()
    for i, pair in enumerate(related):
        values = [
            (matmul(noncore[...], p[...]) * scale).astype(jnp.bfloat16)
            for p in pair
        ]
        for j in range(2):
            @pl.when(place[count + ahead] == j)
            def _(i=i, j=j, values=values):
                own[:, i * rows:(i + 1) * rows] = values[j]
                send[:, i * rows:(i + 1) * rows] = values[1 - j]

    for copy in copies[:2 * count]:
        copy.wait()
    for start in range(0, columns, 256):
        part = slice(start, start + 256)
        total = None if first else before[:, part]
        for i in range(count):
            product = matmul(pieces[i][...], slabs[i, :, part])
            total = product if total is None else total + product
        if len(outs) == 1:
            outs[0][:, part] = total
        else:
            outs[start // half][:, start % half:start % half + 256] = total.astype(
                outs[start // half].dtype
            )
    for copy in copies[2 * count:]:
        copy.wait()


def absorb(pieces, blocks, inverse, before, noncore, pairs, flag, side, scale, final=False):
    count, rows, columns, markers = len(pieces), pieces[0].shape[1], inverse.shape[-1], noncore.shape[1]
    ahead, fetched = len(blocks) - count, inverse.ndim == 3
    operands = [*pieces, inverse] + [piece for pair in pairs for piece in pair]
    operands += [noncore] if pairs else []
    operands += [] if before is None else [before]
    if final:
        outs = [shape((markers, columns // 2), kind) for kind in (jnp.float32, jnp.bfloat16)]
    else:
        outs = [shape((markers, columns), jnp.float32)]
    outs += [shape((noncore.shape[0], rows * len(pairs)))] * 2 if pairs else []
    outs += [shape((ahead, rows, columns))] if ahead else []
    specs = [whole()] * len(operands)
    specs[count] = whole() if fetched else anywhere()
    return pl.pallas_call(
        functools.partial(absorb_kernel, count, len(pairs), ahead, before is None, scale),
        in_specs=[pl.BlockSpec(memory_space=pltpu.SMEM)] + specs,
        out_specs=[whole()] * len(outs),
        out_shape=outs,
        scratch_shapes=[] if fetched else [
            pltpu.VMEM((count, rows, columns), jnp.bfloat16),
            pltpu.SemaphoreType.DMA((2 * (count + ahead),)),
        ],
        compiler_params=params(),
        cost_estimate=SHORT,
        name="absorb",
    )(jnp.stack(blocks + [flag, side]).astype(jnp.int32), *operands)


def relation_kernel(count, scale, flag, done, noncore, *refs):
    pieces, (own, send) = refs[:2 * count], refs[2 * count:]
    width = pieces[0].shape[1]
    for i in range(count):
        columns = slice(i * width, (i + 1) * width)
        values = [
            (matmul(noncore[...], pieces[2 * i + j][...]) * scale).astype(jnp.bfloat16)
            for j in range(2)
        ]
        for j in range(2):
            @pl.when(flag[0] == j)
            def _(j=j):
                own[:, columns] = values[j]
                send[:, columns] = values[1 - j]


def relate(noncore, pairs, flag, scale, after):
    rows, width = noncore.shape[0], pairs[0][0].shape[1]
    out = shape((rows, width * len(pairs)))
    return pl.pallas_call(
        functools.partial(relation_kernel, len(pairs), scale),
        in_specs=[pl.BlockSpec(memory_space=pltpu.SMEM), anywhere()]
        + [whole()] * (2 * len(pairs) + 1),
        out_specs=(whole(), whole()),
        out_shape=(out, out),
        compiler_params=params(),
        cost_estimate=SHORT,
        name="relate",
    )(flag.astype(jnp.int32)[None], after, noncore, *[piece for pair in pairs for piece in pair])


def regression_kernel(count, scale, flag, kept, got, mine, one, two, *outs):
    rows = outs[0].shape[0]
    for j in range(2):
        left, right = ((mine, one), (one, two))[j]

        @pl.when(flag[0] == j)
        def _(left=left, right=right):
            for k in range(count):
                block = slice(k * rows, (k + 1) * rows)
                value = matmul(kept[block, :], left[...]) + matmul(got[block, :], right[...])
                outs[k][...] = (value * scale).astype(jnp.bfloat16)


def regress(kept, got, mine, one, two, flag, count, scale):
    rows, width = kept.shape[0] // count, mine.shape[1]
    return pl.pallas_call(
        functools.partial(regression_kernel, count, scale),
        in_specs=[pl.BlockSpec(memory_space=pltpu.SMEM)] + [whole()] * 5,
        out_specs=[whole()] * count,
        out_shape=[shape((rows, width))] * count,
        compiler_params=params(),
        cost_estimate=SHORT,
        name="regress",
    )(flag.astype(jnp.int32)[None], kept, got, mine, one, two)


def assemble_kernel(jobs, place, *refs):
    refs, sem = list(refs[:-1]), refs[-1]
    outs = refs[-len(jobs):]
    copies = []
    for (count, width), out in zip(jobs, outs):
        for _ in range(count):
            part = refs.pop(0)
            for start in range(0, part.shape[1], width):
                slot = len(copies)
                columns = pl.ds(pl.multiple_of(place[slot] * width, width), width)
                copies.append(
                    pltpu.make_async_copy(
                        part.at[:, start:start + width], out.at[:, columns], sem.at[slot]
                    )
                )
                copies[-1].start()
    for copy in copies:
        copy.wait()


def assemble(jobs):
    parts = [part for job in jobs for part in job[0]]
    slots = [slot for job in jobs for slot in job[1]]
    return pl.pallas_call(
        functools.partial(assemble_kernel, [(len(job[0]), job[2]) for job in jobs]),
        in_specs=[pl.BlockSpec(memory_space=pltpu.SMEM)] + [anywhere()] * len(parts),
        out_specs=[anywhere()] * len(jobs),
        out_shape=[shape((job[0][0].shape[0], job[2] * len(job[1]))) for job in jobs],
        scratch_shapes=[pltpu.SemaphoreType.DMA((len(slots),))],
        compiler_params=params(),
        cost_estimate=SHORT,
        name="assemble",
    )(jnp.stack(slots).astype(jnp.int32), *parts)


def permute_body(
    noncore_geno, noncore_codes, core_geno, core_codes, breed_freqs, core_inverse, *, n_anim, n_mark
):
    markers = breed_freqs.shape[1]
    scale = 1.0 / (markers * n_mark)
    top = n_anim // 2
    grp, anim, mark = (lax.axis_index(name) for name in AXES)

    def move(array, target):
        pairs = []
        for g in range(2):
            for a in range(n_anim):
                for m in range(2):
                    if to := target(g, a, m):
                        pairs.append(
                            ((g * n_anim + a) * 2 + m, (to[0] * n_anim + to[1]) * 2 + to[2])
                        )
        return lax.ppermute(array, AXES, pairs)

    def along_anim(array, bits):
        return move(array, lambda g, a, m: (g, a ^ bits, m))

    def across_grp(array):
        return move(array, lambda g, a, m: (1 - g, a, m))

    def across_mark(array):
        return move(array, lambda g, a, m: (g, a, 1 - m))

    def after(*arrays):
        return lax.optimization_barrier(arrays)

    own, noncore = centre(
        grp, core_geno, core_codes, breed_freqs, noncore_geno, noncore_codes
    )
    rows = noncore.shape[0]
    both = jnp.concatenate([noncore, across_grp(noncore)], axis=0)
    at_home = mark == anim // top
    flag = jnp.where(at_home, 0, 1)
    inverse = in_hbm(core_inverse)
    pieces, related = {0: own}, []

    def take(chosen, total, pairs=(), ahead=(), rows_of=inverse, final=False):
        result = absorb(
            [pieces[b] for b in chosen], [(anim ^ b) * 2 + grp for b in [*chosen, *ahead]], rows_of,
            total, both, [(pieces[b], pieces[b + top]) for b in pairs], flag, grp,
            scale, final,
        )
        if pairs:
            related.extend(result[1:3])
        return [result[0], *result[3 if pairs else 1:]]

    low = list(range(2, top, 2))
    for bits in [top] + low + [1]:
        pieces[bits] = along_anim(own, bits)
    held = [top, 1]
    *moved, both = after(*[pieces[b] for b in held], both)
    pieces.update(zip(held, moved))
    for bits in low:
        pieces[top + bits] = along_anim(pieces[top], bits)
    pieces[top + 1] = along_anim(pieces[top], 1)
    for bits in low:
        pieces[bits + 1] = along_anim(pieces[bits], 1)
    (total,) = take([0, 1, top] + low, None, [0])
    pieces[top + 1], total = after(pieces[top + 1], total)
    for bits in low:
        pieces[top + bits + 1] = along_anim(pieces[top + 1], bits)

    kept, pieces[top + low[-1]] = after(both, pieces[top + low[-1]])
    beside = along_anim(kept, 1)

    last = [bits + i for bits in low for i in (1, top + 1)]
    total, slabs = take([top + 1] + [top + b for b in low], total, [1] + low, last)
    keep, send = take(last, total, rows_of=slabs, final=True)
    from_other = across_grp(send)

    related += relate(both, [(pieces[b + 1], pieces[top + b + 1]) for b in low], flag, scale, keep)
    beside, related[-1] = after(beside, related[-1])
    kept = jnp.concatenate([kept, beside], axis=0)
    bit = 2
    while bit < top:
        kept = jnp.concatenate([kept, along_anim(kept, bit)], axis=0)
        bit *= 2
    received = [across_mark(part) for part in related[1::2]]
    sums = [
        jnp.concatenate(
            [
                (mine[part].astype(jnp.float32) + yours[part].astype(jnp.float32)).astype(
                    jnp.bfloat16
                )
                for mine, yours in zip(related[::2], received)
            ],
            axis=1,
        )
        for part in (slice(0, rows), slice(rows, 2 * rows))
    ]

    sums[1], from_other = after(sums[1], from_other)
    swapped = across_grp(sums[1])

    mine = (keep + from_other.astype(jnp.float32)).astype(jnp.bfloat16)
    one = move(mine, lambda g, a, m: (g, a ^ top, m) if m == a // top else (g, a, 1 - m))
    two = move(mine, lambda g, a, m: None if m == a // top else (g, a ^ top, 1 - m))

    results = regress(kept, across_mark(kept), mine, one, two, flag, 2 * top, scale)
    step = lambda k: k >> 1
    arrived = [
        results[k] if k == 0 else move(results[k], lambda g, a, m, k=k: (g ^ k & 1, a ^ step(k), m))
        for k in range(2 * top)
    ]
    slots = [((anim ^ step(k)) % top) * 2 + (grp ^ k & 1) for k in range(2 * top)]
    width = mine.shape[1]

    width_of_piece = own.shape[1]
    order = [0, 1] + low + [b + 1 for b in low]
    places = [2 * ((anim ^ b) % top) + g for g in (grp, 1 - grp) for b in order]
    return tuple(
        assemble([([sums[0], swapped], places, width_of_piece), (arrived, slots, width)])
    )


def solution(mesh):
    in_specs = (
        P(("grp", "anim"), "mark"),
        P(None, ("grp", "anim")),
        P("anim", "mark"),
        P(None, "anim"),
        P(None, "mark"),
        P(None, "anim"),
    )
    out_specs = (P(("grp", "anim"), "mark"), P(("grp", "anim"), "mark"))
    n_grp, n_anim, n_mark = (mesh.shape[name] for name in AXES)
    if n_grp == 2 and n_mark == 2 and n_anim in (4, 8, 16):
        body = functools.partial(permute_body, n_anim=n_anim, n_mark=n_mark)
    else:
        body = functools.partial(gather_body, n_mark=n_mark)
    return jax.shard_map(body, mesh=mesh, in_specs=in_specs, out_specs=out_specs, check_vma=False)
```

```python
import functools

import jax
import jax.numpy as jnp
from jax import lax
from jax.experimental import pallas as pl
from jax.experimental.pallas import tpu as pltpu
from jax.sharding import PartitionSpec as P

AXES = ("grp", "anim", "mark")
VMEM_LIMIT = 16 * 1024 * 1024
SHORT = pl.CostEstimate(flops=0, bytes_accessed=0, transcendentals=0)


def whole():
    return pl.BlockSpec(memory_space=pltpu.VMEM)


def anywhere():
    return pl.BlockSpec(memory_space=pl.ANY)


def in_hbm(array):
    return pltpu.with_memory_space_constraint(array, pltpu.HBM)


def params(**more):
    return pltpu.CompilerParams(vmem_limit_bytes=VMEM_LIMIT, **more)


def shape(dims, dtype=jnp.bfloat16):
    return jax.ShapeDtypeStruct(dims, dtype)


def expected_dot(left, right):
    return lax.dot_general(
        left, right, (((0,), (0,)), ((), ())), precision=lax.Precision.HIGHEST,
        preferred_element_type=jnp.float32,
    )


def matmul(left, right):
    return jnp.dot(left, right, preferred_element_type=jnp.float32)


def centre_value(genotypes, breed_codes, breed_freqs):
    fractions = breed_codes.astype(jnp.float32) / 32.0
    expected = expected_dot(fractions, breed_freqs)
    return (genotypes.astype(jnp.float32) - 2.0 * expected).astype(jnp.bfloat16)


def gather_body(noncore_geno, noncore_codes, core_geno, core_codes, breed_freqs, core_inverse, *, n_mark):
    slab = breed_freqs.shape[1] * n_mark
    noncore_z = centre_value(noncore_geno, noncore_codes, breed_freqs)
    core_z = centre_value(core_geno, core_codes, breed_freqs)
    shard_rows = lax.all_gather(core_z, "anim", axis=0, tiled=True)
    related = (
        lax.dot_general(
            noncore_z, shard_rows, (((1,), (1,)), ((), ())), preferred_element_type=jnp.float32
        )
        / slab
    )
    loading = lax.dot_general(
        shard_rows, core_inverse, (((0,), (0,)), ((), ())), preferred_element_type=jnp.float32
    ).astype(jnp.bfloat16)
    scores = matmul(noncore_z, lax.all_gather(loading, "anim", axis=1, tiled=True)) / slab
    return tuple(
        lax.psum_scatter(part.astype(jnp.bfloat16), "mark", scatter_dimension=1, tiled=True)
        for part in (related, scores)
    )


def centre_kernel(
    place, geno, codes, freqs, noncore_geno, noncore_codes, piece, noncore, *scratch
):
    rows, markers = geno.shape[0] // 2, geno.shape[1]
    mine = pl.ds(pl.multiple_of(place[0] * rows, rows), rows)
    here, sem = scratch[:-1], scratch[-1]
    sources = [codes, freqs, noncore_codes, noncore_geno, geno.at[mine, :]]
    copies = [
        pltpu.make_async_copy(source, target, sem.at[i])
        for i, (source, target) in enumerate(zip(sources, here))
    ]
    for copy in copies:
        copy.start()
    for copy in copies[:3]:
        copy.wait()
    codes, freqs, noncore_codes, noncore_geno, geno = here
    expected = expected_dot(freqs[...], codes[:, mine].astype(jnp.float32) / 32.0)
    noncore_expected = expected_dot(noncore_codes[...].astype(jnp.float32) / 32.0, freqs[...])
    copies[3].wait()
    centred = (noncore_geno[...].astype(jnp.float32) - 2.0 * noncore_expected).astype(jnp.bfloat16)
    noncore[...] = centred
    copies[4].wait()
    dosage = geno[...].astype(jnp.float32).T
    piece[...] = (dosage - 2.0 * expected).astype(jnp.bfloat16)


def centre(part, core_geno, core_codes, breed_freqs, noncore_geno, noncore_codes):
    rows, markers = core_geno.shape[0] // 2, core_geno.shape[1]
    noncore = noncore_geno.shape[0]
    operands = [core_geno, core_codes, breed_freqs, noncore_geno, noncore_codes]
    return pl.pallas_call(
        centre_kernel,
        in_specs=[pl.BlockSpec(memory_space=pltpu.SMEM)] + [anywhere()] * 5,
        out_specs=[whole()] * 2,
        out_shape=[shape((markers, rows)), shape((noncore, markers))],
        scratch_shapes=[
            pltpu.VMEM(core_codes.shape, jnp.int32),
            pltpu.VMEM(breed_freqs.shape, jnp.float32),
            pltpu.VMEM(noncore_codes.shape, jnp.int32),
            pltpu.VMEM(noncore_geno.shape, jnp.int32),
            pltpu.VMEM((rows, markers), jnp.int32),
            pltpu.SemaphoreType.DMA((5,)),
        ],
        compiler_params=params(),
        cost_estimate=SHORT,
        name="centre",
    )(part[None], *[in_hbm(operand) for operand in operands])


def absorb_kernel(count, pairs, ahead, first, scale, place, *refs):
    refs = list(refs)
    pieces = [refs.pop(0) for _ in range(count)]
    inverse = refs.pop(0)
    related = [(refs.pop(0), refs.pop(0)) for _ in range(pairs)]
    noncore = refs.pop(0) if pairs else None
    before = None if first else refs.pop(0)
    fetched = inverse.ndim == 3
    slabs, sem = (inverse, None) if fetched else refs[-2:]
    outs = refs if fetched else refs[:-2]
    later = outs.pop() if ahead else None
    own, send = (outs.pop(-2), outs.pop(-1)) if pairs else (None, None)
    rows, columns = pieces[0].shape[1], inverse.shape[-1]

    copies = []
    half = columns // 2
    for i in range(0 if fetched else count + ahead):
        block = pl.ds(pl.multiple_of(place[i] * rows, rows), rows)
        target = slabs.at[i] if i < count else later.at[i - count]
        for j, side in enumerate((place[count + ahead + 1], 1 - place[count + ahead + 1])):
            source = inverse.at[block, pl.ds(pl.multiple_of(side * half, half), half)]
            copies.append(
                pltpu.make_async_copy(
                    source, target.at[:, j * half:(j + 1) * half], sem.at[2 * i + j]
                )
            )
            copies[-1].start()
    for i, pair in enumerate(related):
        values = [
            (matmul(noncore[...], p[...]) * scale).astype(jnp.bfloat16)
            for p in pair
        ]
        for j in range(2):
            @pl.when(place[count + ahead] == j)
            def _(i=i, j=j, values=values):
                own[:, i * rows:(i + 1) * rows] = values[j]
                send[:, i * rows:(i + 1) * rows] = values[1 - j]

    for copy in copies[:2 * count]:
        copy.wait()
    for start in range(0, columns, 256):
        part = slice(start, start + 256)
        total = None if first else before[:, part]
        for i in range(count):
            product = matmul(pieces[i][...], slabs[i, :, part])
            total = product if total is None else total + product
        if len(outs) == 1:
            outs[0][:, part] = total
        else:
            outs[start // half][:, start % half:start % half + 256] = total.astype(
                outs[start // half].dtype
            )
    for copy in copies[2 * count:]:
        copy.wait()


def absorb(pieces, blocks, inverse, before, noncore, pairs, flag, side, scale, final=False):
    count, rows, columns, markers = len(pieces), pieces[0].shape[1], inverse.shape[-1], noncore.shape[1]
    ahead, fetched = len(blocks) - count, inverse.ndim == 3
    operands = [*pieces, inverse] + [piece for pair in pairs for piece in pair]
    operands += [noncore] if pairs else []
    operands += [] if before is None else [before]
    if final:
        outs = [shape((markers, columns // 2), kind) for kind in (jnp.float32, jnp.bfloat16)]
    else:
        outs = [shape((markers, columns), jnp.float32)]
    outs += [shape((noncore.shape[0], rows * len(pairs)))] * 2 if pairs else []
    outs += [shape((ahead, rows, columns))] if ahead else []
    specs = [whole()] * len(operands)
    specs[count] = whole() if fetched else anywhere()
    return pl.pallas_call(
        functools.partial(absorb_kernel, count, len(pairs), ahead, before is None, scale),
        in_specs=[pl.BlockSpec(memory_space=pltpu.SMEM)] + specs,
        out_specs=[whole()] * len(outs),
        out_shape=outs,
        scratch_shapes=[] if fetched else [
            pltpu.VMEM((count, rows, columns), jnp.bfloat16),
            pltpu.SemaphoreType.DMA((2 * (count + ahead),)),
        ],
        compiler_params=params(),
        cost_estimate=SHORT,
        name="absorb",
    )(jnp.stack(blocks + [flag, side]).astype(jnp.int32), *operands)


def regression_kernel(count, scale, flag, kept, got, mine, mine_other, twin, twin_other, *outs):
    rows = outs[0].shape[0]
    for j in range(2):
        left, right = ((mine, mine_other), (twin, twin_other))[j]

        @pl.when(flag[0] == j)
        def _(left=left, right=right):
            for k in range(count):
                block = slice(k * rows, (k + 1) * rows)
                value = matmul(kept[block, :], left[...]) + matmul(got[block, :], right[...])
                outs[k][...] = (value * scale).astype(jnp.bfloat16)


def regress(kept, got, mine, mine_other, twin, twin_other, flag, count, scale):
    rows, width = kept.shape[0] // count, mine.shape[1]
    return pl.pallas_call(
        functools.partial(regression_kernel, count, scale),
        in_specs=[pl.BlockSpec(memory_space=pltpu.SMEM)] + [whole()] * 6,
        out_specs=[whole()] * count,
        out_shape=[shape((rows, width))] * count,
        compiler_params=params(),
        cost_estimate=SHORT,
        name="regress",
    )(flag.astype(jnp.int32)[None], kept, got, mine, mine_other, twin, twin_other)


def assemble_kernel(jobs, place, *refs):
    refs, sem = list(refs[:-1]), refs[-1]
    outs = refs[-len(jobs):]
    copies = []
    for (count, width), out in zip(jobs, outs):
        for _ in range(count):
            part = refs.pop(0)
            for start in range(0, part.shape[1], width):
                slot = len(copies)
                columns = pl.ds(pl.multiple_of(place[slot] * width, width), width)
                copies.append(
                    pltpu.make_async_copy(
                        part.at[:, start:start + width], out.at[:, columns], sem.at[slot]
                    )
                )
                copies[-1].start()
    for copy in copies:
        copy.wait()


def assemble(jobs):
    parts = [part for job in jobs for part in job[0]]
    slots = [slot for job in jobs for slot in job[1]]
    return pl.pallas_call(
        functools.partial(assemble_kernel, [(len(job[0]), job[2]) for job in jobs]),
        in_specs=[pl.BlockSpec(memory_space=pltpu.SMEM)] + [anywhere()] * len(parts),
        out_specs=[anywhere()] * len(jobs),
        out_shape=[shape((job[0][0].shape[0], job[2] * len(job[1]))) for job in jobs],
        scratch_shapes=[pltpu.SemaphoreType.DMA((len(slots),))],
        compiler_params=params(),
        cost_estimate=SHORT,
        name="assemble",
    )(jnp.stack(slots).astype(jnp.int32), *parts)


def permute_body(
    noncore_geno, noncore_codes, core_geno, core_codes, breed_freqs, core_inverse, *, n_anim, n_mark
):
    markers = breed_freqs.shape[1]
    scale = 1.0 / (markers * n_mark)
    top = n_anim // 2
    grp, anim, mark = (lax.axis_index(name) for name in AXES)

    def move(array, target):
        pairs = []
        for g in range(2):
            for a in range(n_anim):
                for m in range(2):
                    if to := target(g, a, m):
                        pairs.append(
                            ((g * n_anim + a) * 2 + m, (to[0] * n_anim + to[1]) * 2 + to[2])
                        )
        return lax.ppermute(array, AXES, pairs)

    def along_anim(array, bits):
        return move(array, lambda g, a, m: (g, a ^ bits, m))

    def across_grp(array):
        return move(array, lambda g, a, m: (1 - g, a, m))

    def across_mark(array):
        return move(array, lambda g, a, m: (g, a, 1 - m))

    def after(*arrays):
        return lax.optimization_barrier(arrays)

    own, noncore = centre(
        grp, core_geno, core_codes, breed_freqs, noncore_geno, noncore_codes
    )
    rows = noncore.shape[0]
    both = jnp.concatenate([noncore, across_grp(noncore)], axis=0)
    at_home = mark == anim // top
    flag = jnp.where(at_home, 0, 1)
    inverse = in_hbm(core_inverse)
    pieces, related = {0: own}, []

    def take(chosen, total, pairs=(), ahead=(), rows_of=inverse, final=False):
        result = absorb(
            [pieces[b] for b in chosen], [(anim ^ b) * 2 + grp for b in [*chosen, *ahead]], rows_of,
            total, both, [(pieces[b], pieces[b + top]) for b in pairs], flag, grp,
            scale, final,
        )
        head = 2 if final else 1
        if pairs:
            related.extend(result[head:head + 2])
        return [*result[:head], *result[head + 2 if pairs else head:]]

    low = list(range(2, top, 2))
    for bits in [*low, 1, top]:
        pieces[bits] = along_anim(own, bits)
    pieces[top], pieces[1], both = after(pieces[top], pieces[1], both)
    for bits in low:
        pieces[top + bits] = along_anim(pieces[top], bits)
    for bits in low:
        pieces[bits + 1] = along_anim(pieces[bits], 1)
    pieces[top + 1] = along_anim(pieces[top], 1)
    (total,) = take([0, 1, top] + low, None, [0])
    pieces[top + 1], total = after(pieces[top + 1], total)
    for bits in low:
        pieces[top + bits + 1] = along_anim(pieces[top + 1], bits)

    waited, pieces[top + low[-1]] = after(both, pieces[top + low[-1]])
    beside = along_anim(waited, 1)

    last = [bits + i for bits in low for i in (1, top + 1)]
    total, slabs = take([top + 1] + [top + b for b in low], total, [1] + low, last)
    keep, send = take(last, total, [b + 1 for b in low], rows_of=slabs, final=True)
    from_other = across_grp(send)

    beside, keep = after(beside, keep)
    kept = jnp.concatenate([both, beside], axis=0)
    bit = 2
    while bit < top:
        kept = jnp.concatenate([kept, along_anim(kept, bit)], axis=0)
        bit *= 2

    mine = (keep + from_other.astype(jnp.float32)).astype(jnp.bfloat16)
    twin = along_anim(mine, top)
    mine_other = across_mark(mine)

    received = [across_mark(part) for part in related[1::2]]
    sums = [
        jnp.concatenate(
            [
                (ours[part].astype(jnp.float32) + theirs[part].astype(jnp.float32)).astype(
                    jnp.bfloat16
                )
                for ours, theirs in zip(related[::2], received)
            ],
            axis=1,
        )
        for part in (slice(0, rows), slice(rows, 2 * rows))
    ]
    sums[1], mine_other = after(sums[1], mine_other)
    swapped = across_grp(sums[1])

    kept, mine_other = after(kept, mine_other)
    results = regress(
        kept, across_mark(kept), mine, mine_other, twin, across_mark(twin), flag, 2 * top, scale
    )
    arrived = {0: results[0]}
    for k in range(1, 2 * top):
        arrived[k] = move(results[k], lambda g, a, m, k=k: (g ^ k & 1, a ^ k >> 1, m))
    arrived = [arrived[k] for k in range(2 * top)]
    slots = [((anim ^ k >> 1) % top) * 2 + (grp ^ k & 1) for k in range(2 * top)]
    width = mine.shape[1]

    width_of_piece = own.shape[1]
    order = [0, 1] + low + [b + 1 for b in low]
    places = [2 * ((anim ^ b) % top) + g for g in (grp, 1 - grp) for b in order]
    return tuple(
        assemble(
            [([sums[0], swapped], places, width_of_piece), (arrived, slots, width)]
        )
    )


def solution(mesh):
    in_specs = (
        P(("grp", "anim"), "mark"),
        P(None, ("grp", "anim")),
        P("anim", "mark"),
        P(None, "anim"),
        P(None, "mark"),
        P(None, "anim"),
    )
    out_specs = (P(("grp", "anim"), "mark"), P(("grp", "anim"), "mark"))
    n_grp, n_anim, n_mark = (mesh.shape[name] for name in AXES)
    if n_grp == 2 and n_mark == 2 and n_anim in (4, 8, 16):
        body = functools.partial(permute_body, n_anim=n_anim, n_mark=n_mark)
    else:
        body = functools.partial(gather_body, n_mark=n_mark)
    return jax.shard_map(body, mesh=mesh, in_specs=in_specs, out_specs=out_specs, check_vma=False)
```

```python
import functools

import jax
import jax.numpy as jnp
from jax import lax
from jax.experimental import pallas as pl
from jax.experimental.pallas import tpu as pltpu
from jax.sharding import PartitionSpec as P

AXES = ("grp", "anim", "mark")
VMEM_LIMIT = 16 * 1024 * 1024
SHORT = pl.CostEstimate(flops=0, bytes_accessed=0, transcendentals=0)


def whole():
    return pl.BlockSpec(memory_space=pltpu.VMEM)


def anywhere():
    return pl.BlockSpec(memory_space=pl.ANY)


def in_hbm(array):
    return pltpu.with_memory_space_constraint(array, pltpu.HBM)


def params(**more):
    return pltpu.CompilerParams(vmem_limit_bytes=VMEM_LIMIT, **more)


def shape(dims, dtype=jnp.bfloat16):
    return jax.ShapeDtypeStruct(dims, dtype)


def expected_dot(left, right):
    return lax.dot_general(
        left, right, (((0,), (0,)), ((), ())), precision=lax.Precision.HIGHEST,
        preferred_element_type=jnp.float32,
    )


def matmul(left, right):
    return jnp.dot(left, right, preferred_element_type=jnp.float32)


def centre_value(genotypes, breed_codes, breed_freqs):
    fractions = breed_codes.astype(jnp.float32) / 32.0
    expected = expected_dot(fractions, breed_freqs)
    return (genotypes.astype(jnp.float32) - 2.0 * expected).astype(jnp.bfloat16)


def gather_body(noncore_geno, noncore_codes, core_geno, core_codes, breed_freqs, core_inverse, *, n_mark):
    slab = breed_freqs.shape[1] * n_mark
    noncore_z = centre_value(noncore_geno, noncore_codes, breed_freqs)
    core_z = centre_value(core_geno, core_codes, breed_freqs)
    shard_rows = lax.all_gather(core_z, "anim", axis=0, tiled=True)
    related = (
        lax.dot_general(
            noncore_z, shard_rows, (((1,), (1,)), ((), ())), preferred_element_type=jnp.float32
        )
        / slab
    )
    loading = lax.dot_general(
        shard_rows, core_inverse, (((0,), (0,)), ((), ())), preferred_element_type=jnp.float32
    ).astype(jnp.bfloat16)
    scores = matmul(noncore_z, lax.all_gather(loading, "anim", axis=1, tiled=True)) / slab
    return tuple(
        lax.psum_scatter(part.astype(jnp.bfloat16), "mark", scatter_dimension=1, tiled=True)
        for part in (related, scores)
    )


def centre_kernel(
    place, geno, codes, freqs, noncore_geno, noncore_codes, piece, noncore, *scratch
):
    rows, markers = geno.shape[0] // 2, geno.shape[1]
    mine = pl.ds(pl.multiple_of(place[0] * rows, rows), rows)
    here, sem = scratch[:-1], scratch[-1]
    sources = [codes, freqs, noncore_codes, noncore_geno, geno.at[mine, :]]
    copies = [
        pltpu.make_async_copy(source, target, sem.at[i])
        for i, (source, target) in enumerate(zip(sources, here))
    ]
    for copy in copies:
        copy.start()
    for copy in copies[:3]:
        copy.wait()
    codes, freqs, noncore_codes, noncore_geno, geno = here
    expected = expected_dot(freqs[...], codes[:, mine].astype(jnp.float32) / 32.0)
    noncore_expected = expected_dot(noncore_codes[...].astype(jnp.float32) / 32.0, freqs[...])
    copies[3].wait()
    centred = (noncore_geno[...].astype(jnp.float32) - 2.0 * noncore_expected).astype(jnp.bfloat16)
    noncore[...] = centred
    copies[4].wait()
    dosage = geno[...].astype(jnp.float32).T
    piece[...] = (dosage - 2.0 * expected).astype(jnp.bfloat16)


def centre(part, core_geno, core_codes, breed_freqs, noncore_geno, noncore_codes):
    rows, markers = core_geno.shape[0] // 2, core_geno.shape[1]
    noncore = noncore_geno.shape[0]
    operands = [core_geno, core_codes, breed_freqs, noncore_geno, noncore_codes]
    return pl.pallas_call(
        centre_kernel,
        in_specs=[pl.BlockSpec(memory_space=pltpu.SMEM)] + [anywhere()] * 5,
        out_specs=[whole()] * 2,
        out_shape=[shape((markers, rows)), shape((noncore, markers))],
        scratch_shapes=[
            pltpu.VMEM(core_codes.shape, jnp.int32),
            pltpu.VMEM(breed_freqs.shape, jnp.float32),
            pltpu.VMEM(noncore_codes.shape, jnp.int32),
            pltpu.VMEM(noncore_geno.shape, jnp.int32),
            pltpu.VMEM((rows, markers), jnp.int32),
            pltpu.SemaphoreType.DMA((5,)),
        ],
        compiler_params=params(),
        cost_estimate=SHORT,
        name="centre",
    )(part[None], *[in_hbm(operand) for operand in operands])


def absorb_kernel(count, pairs, ahead, first, scale, place, *refs):
    refs = list(refs)
    pieces = [refs.pop(0) for _ in range(count)]
    inverse = refs.pop(0)
    related = [(refs.pop(0), refs.pop(0)) for _ in range(pairs)]
    noncore = refs.pop(0) if pairs else None
    before = None if first else refs.pop(0)
    fetched = inverse.ndim == 3
    slabs, sem = (inverse, None) if fetched else refs[-2:]
    outs = refs if fetched else refs[:-2]
    later = outs.pop() if ahead else None
    own, send = (outs.pop(-2), outs.pop(-1)) if pairs else (None, None)
    rows, columns = pieces[0].shape[1], inverse.shape[-1]

    copies = []
    half = columns // 2
    for i in range(0 if fetched else count + ahead):
        block = pl.ds(pl.multiple_of(place[i] * rows, rows), rows)
        target = slabs.at[i] if i < count else later.at[i - count]
        for j, side in enumerate((place[count + ahead + 1], 1 - place[count + ahead + 1])):
            source = inverse.at[block, pl.ds(pl.multiple_of(side * half, half), half)]
            copies.append(
                pltpu.make_async_copy(
                    source, target.at[:, j * half:(j + 1) * half], sem.at[2 * i + j]
                )
            )
            copies[-1].start()
    for i, pair in enumerate(related):
        values = [
            (matmul(noncore[...], p[...]) * scale).astype(jnp.bfloat16)
            for p in pair
        ]
        for j in range(2):
            @pl.when(place[count + ahead] == j)
            def _(i=i, j=j, values=values):
                own[:, i * rows:(i + 1) * rows] = values[j]
                send[:, i * rows:(i + 1) * rows] = values[1 - j]

    for copy in copies[:2 * count]:
        copy.wait()
    for start in range(0, columns, 256):
        part = slice(start, start + 256)
        total = None if first else before[:, part]
        for i in range(count):
            product = matmul(pieces[i][...], slabs[i, :, part])
            total = product if total is None else total + product
        if len(outs) == 1:
            outs[0][:, part] = total
        else:
            outs[start // half][:, start % half:start % half + 256] = total.astype(
                outs[start // half].dtype
            )
    for copy in copies[2 * count:]:
        copy.wait()


def absorb(pieces, blocks, inverse, before, noncore, pairs, flag, side, scale, final=False):
    count, rows, columns, markers = len(pieces), pieces[0].shape[1], inverse.shape[-1], noncore.shape[1]
    ahead, fetched = len(blocks) - count, inverse.ndim == 3
    operands = [*pieces, inverse] + [piece for pair in pairs for piece in pair]
    operands += [noncore] if pairs else []
    operands += [] if before is None else [before]
    if final:
        outs = [shape((markers, columns // 2), kind) for kind in (jnp.float32, jnp.bfloat16)]
    else:
        outs = [shape((markers, columns), jnp.float32)]
    outs += [shape((noncore.shape[0], rows * len(pairs)))] * 2 if pairs else []
    outs += [shape((ahead, rows, columns))] if ahead else []
    specs = [whole()] * len(operands)
    specs[count] = whole() if fetched else anywhere()
    return pl.pallas_call(
        functools.partial(absorb_kernel, count, len(pairs), ahead, before is None, scale),
        in_specs=[pl.BlockSpec(memory_space=pltpu.SMEM)] + specs,
        out_specs=[whole()] * len(outs),
        out_shape=outs,
        scratch_shapes=[] if fetched else [
            pltpu.VMEM((count, rows, columns), jnp.bfloat16),
            pltpu.SemaphoreType.DMA((2 * (count + ahead),)),
        ],
        compiler_params=params(),
        cost_estimate=SHORT,
        name="absorb",
    )(jnp.stack(blocks + [flag, side]).astype(jnp.int32), *operands)


def regression_kernel(count, scale, place, kept, got, mine, mine_other, twin, twin_other, *outs):
    rows = outs[0].shape[0]
    for j in range(2):
        left, right = ((mine, mine_other), (twin, twin_other))[j]

        @pl.when(place[count] == j)
        def _(left=left, right=right):
            for k in range(count):
                block = pl.ds(pl.multiple_of(place[k] * rows, rows), rows)
                value = matmul(kept[block, :], left[...]) + matmul(got[block, :], right[...])
                outs[k][...] = (value * scale).astype(jnp.bfloat16)


def regress(kept, got, mine, mine_other, twin, twin_other, blocks, flag, scale):
    count, width = len(blocks), mine.shape[1]
    rows = kept.shape[0] // count
    return pl.pallas_call(
        functools.partial(regression_kernel, count, scale),
        in_specs=[pl.BlockSpec(memory_space=pltpu.SMEM)] + [whole()] * 6,
        out_specs=[whole()] * count,
        out_shape=[shape((rows, width))] * count,
        compiler_params=params(),
        cost_estimate=SHORT,
        name="regress",
    )(
        jnp.stack([*blocks, flag]).astype(jnp.int32), kept, got, mine, mine_other, twin, twin_other
    )


def assemble_kernel(jobs, place, *refs):
    refs, sem = list(refs[:-1]), refs[-1]
    outs = refs[-len(jobs):]
    copies = []
    for (count, width), out in zip(jobs, outs):
        for _ in range(count):
            part = refs.pop(0)
            for start in range(0, part.shape[1], width):
                slot = len(copies)
                columns = pl.ds(pl.multiple_of(place[slot] * width, width), width)
                copies.append(
                    pltpu.make_async_copy(
                        part.at[:, start:start + width], out.at[:, columns], sem.at[slot]
                    )
                )
                copies[-1].start()
    for copy in copies:
        copy.wait()


def assemble(jobs):
    parts = [part for job in jobs for part in job[0]]
    slots = [slot for job in jobs for slot in job[1]]
    return pl.pallas_call(
        functools.partial(assemble_kernel, [(len(job[0]), job[2]) for job in jobs]),
        in_specs=[pl.BlockSpec(memory_space=pltpu.SMEM)] + [anywhere()] * len(parts),
        out_specs=[anywhere()] * len(jobs),
        out_shape=[shape((job[0][0].shape[0], job[2] * len(job[1]))) for job in jobs],
        scratch_shapes=[pltpu.SemaphoreType.DMA((len(slots),))],
        compiler_params=params(),
        cost_estimate=SHORT,
        name="assemble",
    )(jnp.stack(slots).astype(jnp.int32), *parts)


def permute_body(
    noncore_geno, noncore_codes, core_geno, core_codes, breed_freqs, core_inverse, *, n_anim, n_mark
):
    markers = breed_freqs.shape[1]
    scale = 1.0 / (markers * n_mark)
    top = n_anim // 2
    grp, anim, mark = (lax.axis_index(name) for name in AXES)

    def move(array, target):
        pairs = []
        for g in range(2):
            for a in range(n_anim):
                for m in range(2):
                    if to := target(g, a, m):
                        pairs.append(
                            ((g * n_anim + a) * 2 + m, (to[0] * n_anim + to[1]) * 2 + to[2])
                        )
        return lax.ppermute(array, AXES, pairs)

    def along_anim(array, bits):
        return move(array, lambda g, a, m: (g, a ^ bits, m))

    def across_grp(array):
        return move(array, lambda g, a, m: (1 - g, a, m))

    def across_mark(array):
        return move(array, lambda g, a, m: (g, a, 1 - m))

    def after(*arrays):
        return lax.optimization_barrier(arrays)

    own, noncore = centre(
        grp, core_geno, core_codes, breed_freqs, noncore_geno, noncore_codes
    )
    rows = noncore.shape[0]
    both = jnp.concatenate([noncore, across_grp(noncore)], axis=0)
    at_home = mark == anim // top
    flag = jnp.where(at_home, 0, 1)
    inverse = in_hbm(core_inverse)
    pieces, related = {0: own}, []

    def take(chosen, total, pairs=(), ahead=(), rows_of=inverse, final=False):
        result = absorb(
            [pieces[b] for b in chosen], [(anim ^ b) * 2 + grp for b in [*chosen, *ahead]], rows_of,
            total, both, [(pieces[b], pieces[b + top]) for b in pairs], flag, grp,
            scale, final,
        )
        head = 2 if final else 1
        if pairs:
            related.extend(result[head:head + 2])
        return [*result[:head], *result[head + 2 if pairs else head:]]

    low = list(range(2, top, 2))
    for bits in [*low, 1, top]:
        pieces[bits] = along_anim(own, bits)
    pieces[top], pieces[1], both = after(pieces[top], pieces[1], both)
    for bits in low:
        pieces[top + bits] = along_anim(pieces[top], bits)
    for bits in low:
        pieces[bits + 1] = along_anim(pieces[bits], 1)
    pieces[top + 1] = along_anim(pieces[top], 1)
    (total,) = take([0, 1, top] + low, None, [0])
    pieces[top + 1], total = after(pieces[top + 1], total)
    for bits in low:
        pieces[top + bits + 1] = along_anim(pieces[top + 1], bits)

    waited, pieces[top + low[-1]] = after(both, pieces[top + low[-1]])
    beside = along_anim(waited, 1)

    last = [bits + i for bits in low for i in (1, top + 1)]
    total, slabs = take([top + 1] + [top + b for b in low], total, [1] + low, last)
    keep, send = take(last, total, [b + 1 for b in low], rows_of=slabs, final=True)
    from_other = across_grp(send)

    beside, keep = after(beside, keep)
    kept = jnp.concatenate([both, beside], axis=0)
    bit = 2
    while bit < top:
        kept = jnp.concatenate([kept, along_anim(kept, bit)], axis=0)
        bit *= 2

    mine = (keep + from_other.astype(jnp.float32)).astype(jnp.bfloat16)
    twin = along_anim(mine, top)
    mine_other = across_mark(mine)

    received = [across_mark(part) for part in related[1::2]]
    sums = [
        jnp.concatenate(
            [
                (ours[part].astype(jnp.float32) + theirs[part].astype(jnp.float32)).astype(
                    jnp.bfloat16
                )
                for ours, theirs in zip(related[::2], received)
            ],
            axis=1,
        )
        for part in (slice(0, rows), slice(rows, 2 * rows))
    ]
    sums[1], mine_other = after(sums[1], mine_other)
    swapped = across_grp(sums[1])

    size = 2 * top
    steps = [sorted(range(size), key=lambda k: (k.bit_count(), k))]
    steps.append([(k >> 1 | k << size.bit_length() - 2) & size - 1 for k in steps[0]])
    step = [jnp.where(mark == 0, k, l) for k, l in zip(*steps)]
    kept, mine_other = after(kept, mine_other)
    results = regress(
        kept, across_mark(kept), mine, mine_other, twin, across_mark(twin), step, flag, scale
    )
    arrived = [results[0]]
    for i in range(1, size):
        arrived.append(
            move(results[i], lambda g, a, m: (g ^ steps[m][i] & 1, a ^ steps[m][i] >> 1, m))
        )
    slots = [((anim ^ (k >> 1)) % top) * 2 + (grp ^ (k & 1)) for k in step]
    width = mine.shape[1]

    width_of_piece = own.shape[1]
    order = [0, 1] + low + [b + 1 for b in low]
    places = [2 * ((anim ^ b) % top) + g for g in (grp, 1 - grp) for b in order]
    return tuple(
        assemble(
            [([sums[0], swapped], places, width_of_piece), (arrived, slots, width)]
        )
    )


def solution(mesh):
    in_specs = (
        P(("grp", "anim"), "mark"),
        P(None, ("grp", "anim")),
        P("anim", "mark"),
        P(None, "anim"),
        P(None, "mark"),
        P(None, "anim"),
    )
    out_specs = (P(("grp", "anim"), "mark"), P(("grp", "anim"), "mark"))
    n_grp, n_anim, n_mark = (mesh.shape[name] for name in AXES)
    if n_grp == 2 and n_mark == 2 and n_anim in (4, 8, 16):
        body = functools.partial(permute_body, n_anim=n_anim, n_mark=n_mark)
    else:
        body = functools.partial(gather_body, n_mark=n_mark)
    return jax.shard_map(body, mesh=mesh, in_specs=in_specs, out_specs=out_specs, check_vma=False)
```

```python
import functools

import jax
import jax.numpy as jnp
from jax import lax
from jax.experimental import pallas as pl
from jax.experimental.pallas import tpu as pltpu
from jax.sharding import PartitionSpec as P

AXES = ("grp", "anim", "mark")
VMEM_LIMIT = 16 * 1024 * 1024
SHORT = pl.CostEstimate(flops=0, bytes_accessed=0, transcendentals=0)


def whole():
    return pl.BlockSpec(memory_space=pltpu.VMEM)


def anywhere():
    return pl.BlockSpec(memory_space=pl.ANY)


def in_hbm(array):
    return pltpu.with_memory_space_constraint(array, pltpu.HBM)


def params(**more):
    return pltpu.CompilerParams(vmem_limit_bytes=VMEM_LIMIT, **more)


def shape(dims, dtype=jnp.bfloat16):
    return jax.ShapeDtypeStruct(dims, dtype)


def expected_dot(left, right):
    return lax.dot_general(
        left, right, (((0,), (0,)), ((), ())), precision=lax.Precision.HIGHEST,
        preferred_element_type=jnp.float32,
    )


def matmul(left, right):
    return jnp.dot(left, right, preferred_element_type=jnp.float32)


def centre_value(genotypes, breed_codes, breed_freqs):
    fractions = breed_codes.astype(jnp.float32) / 32.0
    expected = expected_dot(fractions, breed_freqs)
    return (genotypes.astype(jnp.float32) - 2.0 * expected).astype(jnp.bfloat16)


def gather_body(noncore_geno, noncore_codes, core_geno, core_codes, breed_freqs, core_inverse, *, n_mark):
    slab = breed_freqs.shape[1] * n_mark
    noncore_z = centre_value(noncore_geno, noncore_codes, breed_freqs)
    core_z = centre_value(core_geno, core_codes, breed_freqs)
    shard_rows = lax.all_gather(core_z, "anim", axis=0, tiled=True)
    related = (
        lax.dot_general(
            noncore_z, shard_rows, (((1,), (1,)), ((), ())), preferred_element_type=jnp.float32
        )
        / slab
    )
    loading = lax.dot_general(
        shard_rows, core_inverse, (((0,), (0,)), ((), ())), preferred_element_type=jnp.float32
    ).astype(jnp.bfloat16)
    scores = matmul(noncore_z, lax.all_gather(loading, "anim", axis=1, tiled=True)) / slab
    return tuple(
        lax.psum_scatter(part.astype(jnp.bfloat16), "mark", scatter_dimension=1, tiled=True)
        for part in (related, scores)
    )


def centre_kernel(
    place, geno, codes, freqs, noncore_geno, noncore_codes, piece, noncore, *scratch
):
    rows, markers = geno.shape[0] // 2, geno.shape[1]
    mine = pl.ds(pl.multiple_of(place[0] * rows, rows), rows)
    here, sem = scratch[:-1], scratch[-1]
    sources = [codes, freqs, noncore_codes, noncore_geno, geno.at[mine, :]]
    copies = [
        pltpu.make_async_copy(source, target, sem.at[i])
        for i, (source, target) in enumerate(zip(sources, here))
    ]
    for copy in copies:
        copy.start()
    for copy in copies[:3]:
        copy.wait()
    codes, freqs, noncore_codes, noncore_geno, geno = here
    expected = expected_dot(freqs[...], codes[:, mine].astype(jnp.float32) / 32.0)
    noncore_expected = expected_dot(noncore_codes[...].astype(jnp.float32) / 32.0, freqs[...])
    copies[3].wait()
    centred = (noncore_geno[...].astype(jnp.float32) - 2.0 * noncore_expected).astype(jnp.bfloat16)
    noncore[...] = centred
    copies[4].wait()
    dosage = geno[...].astype(jnp.bfloat16).T.astype(jnp.float32)
    piece[...] = (dosage - 2.0 * expected).astype(jnp.bfloat16)


def centre(part, core_geno, core_codes, breed_freqs, noncore_geno, noncore_codes):
    rows, markers = core_geno.shape[0] // 2, core_geno.shape[1]
    noncore = noncore_geno.shape[0]
    operands = [core_geno, core_codes, breed_freqs, noncore_geno, noncore_codes]
    return pl.pallas_call(
        centre_kernel,
        in_specs=[pl.BlockSpec(memory_space=pltpu.SMEM)] + [anywhere()] * 5,
        out_specs=[whole()] * 2,
        out_shape=[shape((markers, rows)), shape((noncore, markers))],
        scratch_shapes=[
            pltpu.VMEM(core_codes.shape, jnp.int32),
            pltpu.VMEM(breed_freqs.shape, jnp.float32),
            pltpu.VMEM(noncore_codes.shape, jnp.int32),
            pltpu.VMEM(noncore_geno.shape, jnp.int32),
            pltpu.VMEM((rows, markers), jnp.int32),
            pltpu.SemaphoreType.DMA((5,)),
        ],
        compiler_params=params(),
        cost_estimate=SHORT,
        name="centre",
    )(part[None], *[in_hbm(operand) for operand in operands])


def absorb_kernel(count, pairs, ahead, first, scale, place, *refs):
    refs = list(refs)
    pieces = [refs.pop(0) for _ in range(count)]
    inverse = refs.pop(0)
    related = [(refs.pop(0), refs.pop(0)) for _ in range(pairs)]
    noncore = refs.pop(0) if pairs else None
    before = None if first else refs.pop(0)
    fetched = inverse.ndim == 3
    slabs, sem = (inverse, None) if fetched else refs[-2:]
    outs = refs if fetched else refs[:-2]
    later = outs.pop() if ahead else None
    own, send = (outs.pop(-2), outs.pop(-1)) if pairs else (None, None)
    rows, columns = pieces[0].shape[1], inverse.shape[-1]

    copies = []
    half = columns // 2
    for i in range(0 if fetched else count + ahead):
        block = pl.ds(pl.multiple_of(place[i] * rows, rows), rows)
        target = slabs.at[i] if i < count else later.at[i - count]
        for j, side in enumerate((place[count + ahead + 1], 1 - place[count + ahead + 1])):
            source = inverse.at[block, pl.ds(pl.multiple_of(side * half, half), half)]
            copies.append(
                pltpu.make_async_copy(
                    source, target.at[:, j * half:(j + 1) * half], sem.at[2 * i + j]
                )
            )
            copies[-1].start()
    for i, pair in enumerate(related):
        values = [
            (matmul(noncore[...], p[...]) * scale).astype(jnp.bfloat16)
            for p in pair
        ]
        for j in range(2):
            @pl.when(place[count + ahead] == j)
            def _(i=i, j=j, values=values):
                own[:, i * rows:(i + 1) * rows] = values[j]
                send[:, i * rows:(i + 1) * rows] = values[1 - j]

    for copy in copies[:2 * count]:
        copy.wait()
    for start in range(0, columns, 256):
        part = slice(start, start + 256)
        total = None if first else before[:, part]
        for i in range(count):
            product = matmul(pieces[i][...], slabs[i, :, part])
            total = product if total is None else total + product
        if len(outs) == 1:
            outs[0][:, part] = total
        else:
            outs[start // half][:, start % half:start % half + 256] = total.astype(
                outs[start // half].dtype
            )
    for copy in copies[2 * count:]:
        copy.wait()


def absorb(pieces, blocks, inverse, before, noncore, pairs, flag, side, scale, final=False):
    count, rows, columns, markers = len(pieces), pieces[0].shape[1], inverse.shape[-1], noncore.shape[1]
    ahead, fetched = len(blocks) - count, inverse.ndim == 3
    operands = [*pieces, inverse] + [piece for pair in pairs for piece in pair]
    operands += [noncore] if pairs else []
    operands += [] if before is None else [before]
    if final:
        outs = [shape((markers, columns // 2), kind) for kind in (jnp.float32, jnp.bfloat16)]
    else:
        outs = [shape((markers, columns), jnp.float32)]
    outs += [shape((noncore.shape[0], rows * len(pairs)))] * 2 if pairs else []
    outs += [shape((ahead, rows, columns))] if ahead else []
    specs = [whole()] * len(operands)
    specs[count] = whole() if fetched else anywhere()
    return pl.pallas_call(
        functools.partial(absorb_kernel, count, len(pairs), ahead, before is None, scale),
        in_specs=[pl.BlockSpec(memory_space=pltpu.SMEM)] + specs,
        out_specs=[whole()] * len(outs),
        out_shape=outs,
        scratch_shapes=[] if fetched else [
            pltpu.VMEM((count, rows, columns), jnp.bfloat16),
            pltpu.SemaphoreType.DMA((2 * (count + ahead),)),
        ],
        compiler_params=params(),
        cost_estimate=SHORT,
        name="absorb",
    )(jnp.stack(blocks + [flag, side]).astype(jnp.int32), *operands)


def regression_kernel(orders, scale, place, kept, got, mine, mine_other, twin, twin_other, *outs):
    rows = outs[0].shape[0]
    for i, order in enumerate(orders):
        for j, (left, right) in enumerate(((mine, mine_other), (twin, twin_other))):
            @pl.when((place[0] == i) & (place[1] == j))
            def _(order=order, left=left, right=right):
                for out, k in zip(outs, order):
                    block = slice(k * rows, (k + 1) * rows)
                    value = matmul(kept[block, :], left[...]) + matmul(got[block, :], right[...])
                    out[...] = (value * scale).astype(jnp.bfloat16)


def regress(kept, got, mine, mine_other, twin, twin_other, orders, core, flag, scale):
    count, width = len(orders[0]), mine.shape[1]
    rows = kept.shape[0] // count
    return pl.pallas_call(
        functools.partial(regression_kernel, orders, scale),
        in_specs=[pl.BlockSpec(memory_space=pltpu.SMEM)] + [whole()] * 6,
        out_specs=[whole()] * count,
        out_shape=[shape((rows, width))] * count,
        compiler_params=params(),
        cost_estimate=SHORT,
        name="regress",
    )(jnp.stack([core, flag]).astype(jnp.int32), kept, got, mine, mine_other, twin, twin_other)


def assemble_kernel(jobs, place, *refs):
    refs, sem = list(refs[:-1]), refs[-1]
    outs = refs[-len(jobs):]
    copies = []
    for (count, width), out in zip(jobs, outs):
        for _ in range(count):
            part = refs.pop(0)
            for start in range(0, part.shape[1], width):
                slot = len(copies)
                columns = pl.ds(pl.multiple_of(place[slot] * width, width), width)
                copies.append(
                    pltpu.make_async_copy(
                        part.at[:, start:start + width], out.at[:, columns], sem.at[slot]
                    )
                )
                copies[-1].start()
    for copy in copies:
        copy.wait()


def assemble(jobs):
    parts = [part for job in jobs for part in job[0]]
    slots = [slot for job in jobs for slot in job[1]]
    return pl.pallas_call(
        functools.partial(assemble_kernel, [(len(job[0]), job[2]) for job in jobs]),
        in_specs=[pl.BlockSpec(memory_space=pltpu.SMEM)] + [anywhere()] * len(parts),
        out_specs=[anywhere()] * len(jobs),
        out_shape=[shape((job[0][0].shape[0], job[2] * len(job[1]))) for job in jobs],
        scratch_shapes=[pltpu.SemaphoreType.DMA((len(slots),))],
        compiler_params=params(),
        cost_estimate=SHORT,
        name="assemble",
    )(jnp.stack(slots).astype(jnp.int32), *parts)


def permute_body(
    noncore_geno, noncore_codes, core_geno, core_codes, breed_freqs, core_inverse, *, n_anim, n_mark
):
    markers = breed_freqs.shape[1]
    scale = 1.0 / (markers * n_mark)
    top = n_anim // 2
    grp, anim, mark = (lax.axis_index(name) for name in AXES)

    def move(array, target):
        pairs = []
        for g in range(2):
            for a in range(n_anim):
                for m in range(2):
                    if to := target(g, a, m):
                        pairs.append(
                            ((g * n_anim + a) * 2 + m, (to[0] * n_anim + to[1]) * 2 + to[2])
                        )
        return lax.ppermute(array, AXES, pairs)

    def along_anim(array, bits):
        return move(array, lambda g, a, m: (g, a ^ bits, m))

    def across_grp(array):
        return move(array, lambda g, a, m: (1 - g, a, m))

    def across_mark(array):
        return move(array, lambda g, a, m: (g, a, 1 - m))

    def after(*arrays):
        return lax.optimization_barrier(arrays)

    own, noncore = centre(
        grp, core_geno, core_codes, breed_freqs, noncore_geno, noncore_codes
    )
    rows = noncore.shape[0]
    both = jnp.concatenate([noncore, across_grp(noncore)], axis=0)
    at_home = mark == anim // top
    flag = jnp.where(at_home, 0, 1)
    inverse = in_hbm(core_inverse)
    pieces, related = {0: own}, []

    def take(chosen, total, pairs=(), ahead=(), rows_of=inverse, final=False):
        result = absorb(
            [pieces[b] for b in chosen], [(anim ^ b) * 2 + grp for b in [*chosen, *ahead]], rows_of,
            total, both, [(pieces[b], pieces[b + top]) for b in pairs], flag, grp,
            scale, final,
        )
        head = 2 if final else 1
        if pairs:
            related.extend(result[head:head + 2])
        return [*result[:head], *result[head + 2 if pairs else head:]]

    low = list(range(2, top, 2))
    for bits in [*low, 1, top]:
        pieces[bits] = along_anim(own, bits)
    pieces[top], pieces[1], both = after(pieces[top], pieces[1], both)
    for bits in low:
        pieces[top + bits] = along_anim(pieces[top], bits)
    for bits in low:
        pieces[bits + 1] = along_anim(pieces[bits], 1)
    pieces[top + 1] = along_anim(pieces[top], 1)
    (total,) = take([0, 1, top] + low, None, [0])
    pieces[top + 1], total = after(pieces[top + 1], total)
    for bits in low:
        pieces[top + bits + 1] = along_anim(pieces[top + 1], bits)

    waited, pieces[top + low[-1]] = after(both, pieces[top + low[-1]])
    beside = along_anim(waited, 1)

    last = [bits + i for bits in low for i in (1, top + 1)]
    total, slabs = take([top + 1] + [top + b for b in low], total, [1] + low, last)
    keep, send = take(last, total, [b + 1 for b in low], rows_of=slabs, final=True)
    from_other = across_grp(send)

    beside, keep = after(beside, keep)
    kept = jnp.concatenate([both, beside], axis=0)
    bit = 2
    while bit < top:
        kept = jnp.concatenate([kept, along_anim(kept, bit)], axis=0)
        bit *= 2

    mine = (keep + from_other.astype(jnp.float32)).astype(jnp.bfloat16)
    twin = along_anim(mine, top)
    mine_other = across_mark(mine)

    received = [across_mark(part) for part in related[1::2]]
    sums = [
        jnp.concatenate(
            [
                (ours[part].astype(jnp.float32) + theirs[part].astype(jnp.float32)).astype(
                    jnp.bfloat16
                )
                for ours, theirs in zip(related[::2], received)
            ],
            axis=1,
        )
        for part in (slice(0, rows), slice(rows, 2 * rows))
    ]
    sums[1], mine_other = after(sums[1], mine_other)
    swapped = across_grp(sums[1])

    size = 2 * top
    steps = [sorted(range(size), key=lambda k: (k.bit_count(), k))]
    steps.append([(k >> 1 | k << size.bit_length() - 2) & size - 1 for k in steps[0]])
    step = [jnp.where(mark == 0, k, l) for k, l in zip(*steps)]
    kept, mine_other = after(kept, mine_other)
    results = regress(
        kept, across_mark(kept), mine, mine_other, twin, across_mark(twin), steps, mark, flag, scale
    )
    arrived = [results[0]]
    for i in range(1, size):
        arrived.append(
            move(results[i], lambda g, a, m: (g ^ steps[m][i] & 1, a ^ steps[m][i] >> 1, m))
        )
    slots = [((anim ^ (k >> 1)) % top) * 2 + (grp ^ (k & 1)) for k in step]
    width = mine.shape[1]

    width_of_piece = own.shape[1]
    order = [0, 1] + low + [b + 1 for b in low]
    places = [2 * ((anim ^ b) % top) + g for g in (grp, 1 - grp) for b in order]
    return tuple(
        assemble(
            [([sums[0], swapped], places, width_of_piece), (arrived, slots, width)]
        )
    )


def solution(mesh):
    in_specs = (
        P(("grp", "anim"), "mark"),
        P(None, ("grp", "anim")),
        P("anim", "mark"),
        P(None, "anim"),
        P(None, "mark"),
        P(None, "anim"),
    )
    out_specs = (P(("grp", "anim"), "mark"), P(("grp", "anim"), "mark"))
    n_grp, n_anim, n_mark = (mesh.shape[name] for name in AXES)
    if n_grp == 2 and n_mark == 2 and n_anim in (4, 8, 16):
        body = functools.partial(permute_body, n_anim=n_anim, n_mark=n_mark)
    else:
        body = functools.partial(gather_body, n_mark=n_mark)
    return jax.shard_map(body, mesh=mesh, in_specs=in_specs, out_specs=out_specs, check_vma=False)
```
